32 devices in a mesh: grp: 2 (over y), mix: 4 (over z), ffn: 2 (over x), pair: 2 (over core).
Axes of the slice: x: 2, y: 2, z: 4, core: 2. Of those that a mesh axis runs over, the one named last changes fastest.
Arguments:
- query: bfloat16 [512, 8192], P(('grp', 'ffn', 'pair'), 'mix'), parts along dimension 0, may hold values from -100 to 100
- new_key: bfloat16 [512, 8192], P(('grp', 'ffn', 'pair'), 'mix'), parts along dimension 0, may hold values from -6 to 6
- new_value: bfloat16 [512, 8192], P(('grp', 'ffn', 'pair'), 'mix'), parts along dimension 0, may hold values from -6 to 6
- key_cache: bfloat16 [512, 32, 8192], P(('grp', 'ffn', 'pair'), None, 'mix'), parts along dimension 0, may hold values from -6 to 6
- value_cache: bfloat16 [512, 32, 8192], P(('grp', 'ffn', 'pair'), None, 'mix'), parts along dimension 0, may hold values from -6 to 6
- lengths: int32 [512], P(('grp', 'ffn', 'pair')), parts along dimension 0, may hold values from 2 to 32, as said below
- counts: int32 [8], P(('grp', 'ffn', 'pair')), parts along dimension 0, may hold values from 32 to 64, as said below
- residual: bfloat16 [512, 8192], P(('grp', 'ffn', 'pair'), 'mix'), parts along dimension 0, may hold values from -30 to 30
- norm_gain: bfloat16 [8192], P('mix'), may hold values from 0.5 to 1.5
- w_gate: bfloat16 [8192, 21888], P('mix', ('ffn', 'pair')), may hold values from -0.0625 to 0.0625
- w_up: bfloat16 [8192, 21888], P('mix', ('ffn', 'pair')), may hold values from -0.0625 to 0.0625
- w_down: bfloat16 [21888, 8192], P(('ffn', 'pair'), 'mix'), may hold values from -0.0390625 to 0.0390625
Outputs:
- block_out: bfloat16 [512, 8192], P(('grp', 'ffn', 'pair'), 'mix'), parts along dimension 0
The draws below stay inside these ranges and needn't reach their ends.
There are 2 independent parts, one for each index of `grp`. The reference program is written for one: setup_inputs(seed, part) draws one part's arguments, and reference() takes and returns one part's arrays. A program takes and returns all parts, laid end to end along the dimension named above; an argument that names none is the same for every part. Nothing has to cross between parts.
Inputs may be any that keep to these rules, and one draw needn't show every extreme that they name: `counts`: candidate slots beyond a block's count are empty; some block is full. `lengths`: some candidate has 32 cached positions.
All inputs are finite; a program needn't handle non-finite values.
Results may differ from the reference program's by a relative error of at most 0.014.
Values may be sent and summed in bfloat16 or wider, within the bound.
No kernel may reach another device: no remote copies, remote signals or barrier semaphores. Data moves between devices by JAX's collectives and lax.ppermute only.
A program may use at most 192 MiB of HBM per device.

```python
import jax
import jax.numpy as jnp
from jax import lax

D = 8192
FF = 21888
HD = 128
CAND_DEV = 64
LMAX = 32
GROUPS = 4
CANDS = 256
N_MIX = 4


def cache_keys(key):
    base = jnp.clip(jax.random.normal(key, (CANDS, LMAX, D), jnp.float32), -6.0, 6.0)
    second = base[:, 1, :]
    return base.at[:, 1, :].set(second)


def draw_key_cache(key, part):
    keys = cache_keys(key)
    return keys.astype(jnp.bfloat16)


def draw_query(key, part):
    key = jax.random.fold_in(key, 5)
    query = jnp.clip(jax.random.normal(key, (CANDS, D), jnp.float32), -6.0, 6.0)
    return jnp.clip(query, -100.0, 100.0).astype(jnp.bfloat16)


def draw_residual(key, part):
    key = jax.random.fold_in(key, 7)
    key_one, key_two, key_three = jax.random.split(key, 3)
    ramp = jnp.arange(D, dtype=jnp.float32) / D
    column = 10.0 ** (ramp - 1.0) * 2.0 ** (jax.random.uniform(key_two, (D,), jnp.float32) - 0.5)
    row_scale = 10.0 ** (jax.random.uniform(key_three, (CANDS, 1), jnp.float32) - 0.5)
    entries = jnp.clip(jax.random.normal(key_one, (CANDS, D), jnp.float32), -6.0, 6.0)
    return jnp.clip(entries * row_scale * column[None, :], -30.0, 30.0).astype(jnp.bfloat16)


def draw_lengths(key, part):
    key = jax.random.fold_in(key, 9)
    key_one, key_two = jax.random.split(key)
    lengths = jax.random.randint(key_one, (CANDS,), 2, LMAX + 1, jnp.int32)
    chosen = jax.random.randint(key_two, (), 0, CANDS, jnp.int32)
    return lengths.at[chosen].set(LMAX)


def draw_counts(key, part):
    key = jax.random.fold_in(key, 13)
    key_one, key_two = jax.random.split(key)
    counts = jax.random.randint(key_one, (GROUPS,), max(CAND_DEV // 2, 1), CAND_DEV + 1, jnp.int32)
    chosen = jax.random.randint(key_two, (), 0, GROUPS, jnp.int32)
    return counts.at[chosen].set(CAND_DEV)


def block_levels(rng, extent, shards, low, top_value):
    loudness, own = 1.0, jax.random.fold_in(rng, 6)
    for position, blocks in shards:
        heights = jnp.exp(jax.random.uniform(jax.random.fold_in(own, position), (blocks,), jnp.float32, low / len(shards), top_value / len(shards)))
        loudness = loudness * jnp.repeat(heights, extent[position] // blocks).reshape([-1 if axis == position else 1 for axis in range(len(extent))])
    return loudness


def normal_values(rng, dims, width, limit, cuts=(), held_as=jnp.bfloat16):
    array = jax.random.normal(rng, dims, jnp.float32) * width
    if len(cuts) > 0:
        array = block_levels(rng, dims, cuts, -0.22, 0.18) * array
    return jnp.clip(array, min=-limit, max=limit).astype(held_as)


def setup_inputs(seed: int = 0, part: int = 0) -> dict:
    seeds = jax.random.split(jax.random.key(seed), 13)
    own_keys = jax.random.split(jax.random.fold_in(seeds[12], part), 13)
    return {
        "query": draw_query(jax.random.fold_in(jax.random.fold_in(seeds[12], part), 71), part),
        "new_key": normal_values(own_keys[1], (CANDS, D), 1.0, 6.0, ((0, 4), (1, 4))),
        "new_value": normal_values(own_keys[2], (CANDS, D), 1.0, 6.0, ((0, 4), (1, 4))),
        "key_cache": draw_key_cache(jax.random.fold_in(jax.random.fold_in(seeds[12], part), 71), part),
        "value_cache": normal_values(own_keys[4], (CANDS, LMAX, D), 1.0, 6.0, ((0, 4), (2, 4))),
        "lengths": draw_lengths(jax.random.fold_in(jax.random.fold_in(seeds[12], part), 71), part),
        "counts": draw_counts(jax.random.fold_in(jax.random.fold_in(seeds[12], part), 71), part),
        "residual": draw_residual(jax.random.fold_in(jax.random.fold_in(seeds[12], part), 71), part),
        "norm_gain": jnp.clip(1.0 + 0.1 * jax.random.normal(seeds[8], (D,), jnp.float32), 0.5, 1.5).astype(jnp.bfloat16),
        "w_gate": normal_values(seeds[9], (D, FF), D ** -0.5, 0.0625, ((0, 4), (1, 4))),
        "w_up": normal_values(seeds[10], (D, FF), D ** -0.5, 0.0625, ((0, 4), (1, 4))),
        "w_down": normal_values(seeds[11], (FF, D), FF ** -0.5, 0.0390625, ((0, 4), (1, 4))),
    }


eps = 1e-05

def attend(query, new_key, new_value, key_cache, value_cache, lengths):
    rows = query.shape[0]
    heads = query.shape[1] // HD
    cache_len = key_cache.shape[1]
    scale = 1.0 / HD ** 0.5
    q_heads = query.astype(jnp.float32).reshape(rows, heads, HD)
    k_own = new_key.astype(jnp.float32).reshape(rows, heads, HD)
    v_own = new_value.astype(jnp.float32).reshape(rows, heads, HD)
    k_all = key_cache.astype(jnp.float32).reshape(rows, cache_len, heads, HD)
    scores = jnp.einsum('chd,cphd->chp', q_heads, k_all) * scale
    own = lax.optimization_barrier(jnp.sum(q_heads * k_own, axis=-1)) * scale
    valid = jnp.arange(cache_len, dtype=jnp.int32)[None, :] < lengths[:, None]
    scores = jnp.where(valid[:, None, :], scores, -jnp.inf)
    top = jnp.maximum(lax.optimization_barrier(jnp.max(scores, axis=-1)), own)
    weights = jnp.exp(scores - top[..., None])
    own_w = jnp.exp(own - top)
    total = lax.optimization_barrier(jnp.sum(weights, axis=-1)) + own_w
    probs = lax.optimization_barrier((weights / total[..., None]).astype(jnp.bfloat16))
    own_p = lax.optimization_barrier((own_w / total).astype(jnp.bfloat16))
    v_all = value_cache.astype(jnp.float32).reshape(rows, cache_len, heads, HD)
    mixed = jnp.einsum('chp,cphd->chd', probs.astype(jnp.float32), v_all)
    mixed = mixed + own_p.astype(jnp.float32)[..., None] * v_own
    return mixed.reshape(rows, heads * HD)

def reference(query, new_key, new_value, key_cache, value_cache, lengths, counts, residual, norm_gain, w_gate, w_up, w_down):
    mixed = attend(query, new_key, new_value, key_cache, value_cache, lengths)
    x = residual.astype(jnp.float32) + mixed
    ms = lax.optimization_barrier(jnp.sum(x * x, axis=1)) / D
    xn = (x * lax.rsqrt(ms + eps)[:, None] * norm_gain.astype(jnp.float32)).astype(jnp.bfloat16)
    block = D // N_MIX
    pieces_x = xn.reshape(CANDS, N_MIX, block).transpose(1, 0, 2)
    pieces_g = w_gate.reshape(N_MIX, block, FF)
    pieces_u = w_up.reshape(N_MIX, block, FF)

    def accumulate(carry, pieces):
        xpart, gpart, upart = pieces
        part_gate = lax.optimization_barrier(jnp.dot(xpart, gpart, preferred_element_type=jnp.float32).astype(jnp.bfloat16))
        part_up = lax.optimization_barrier(jnp.dot(xpart, upart, preferred_element_type=jnp.float32).astype(jnp.bfloat16))
        return ((carry[0] + part_gate.astype(jnp.float32), carry[1] + part_up.astype(jnp.float32)), None)
    zeros = jnp.zeros((CANDS, FF), jnp.float32)
    (gate, up), _ = lax.scan(accumulate, (zeros, zeros), (pieces_x, pieces_g, pieces_u))
    hidden = (jax.nn.silu(gate) * up).astype(jnp.bfloat16)
    mlp = jnp.dot(hidden, w_down, preferred_element_type=jnp.float32)
    slots = jnp.arange(CANDS, dtype=jnp.int32)
    live = slots % CAND_DEV < jnp.repeat(counts, CAND_DEV)
    return jnp.where(live[:, None], x + mlp, jnp.zeros_like(x)).astype(jnp.bfloat16)
```

```python
import functools

import jax
import jax.numpy as jnp
from jax import lax
from jax.experimental import pallas as pl
from jax.experimental.pallas import tpu as pltpu
from jax.sharding import PartitionSpec as P

D = 8192
HD = 128


eps = 1e-05


def attend(query, new_key, new_value, key_cache, value_cache, lengths):
    rows = query.shape[0]
    heads = query.shape[1] // HD
    cache_len = key_cache.shape[1]
    scale = 1.0 / HD**0.5
    q_heads = query.reshape(rows, heads, HD)
    k_all = key_cache.reshape(rows, cache_len, heads, HD)
    v_all = value_cache.reshape(rows, cache_len, heads, HD)
    scores = jnp.einsum("chd,cphd->chp", q_heads, k_all, preferred_element_type=jnp.float32) * scale
    own = (
        jnp.einsum(
            "chd,chd->ch",
            q_heads,
            new_key.reshape(rows, heads, HD),
            preferred_element_type=jnp.float32,
        )
        * scale
    )
    valid = jnp.arange(cache_len, dtype=jnp.int32)[None, :] < lengths[:, None]
    scores = jnp.where(valid[:, None, :], scores, -jnp.inf)
    top = jnp.maximum(jnp.max(scores, axis=-1), own)
    weights = jnp.exp(scores - top[..., None])
    own_w = jnp.exp(own - top)
    total = jnp.sum(weights, axis=-1) + own_w
    probs = (weights / total[..., None]).astype(jnp.bfloat16)
    own_p = (own_w / total).astype(jnp.bfloat16)
    mixed = jnp.einsum("chp,cphd->chd", probs, v_all, preferred_element_type=jnp.float32)
    own_v = new_value.reshape(rows, heads, HD).astype(jnp.float32)
    mixed = mixed + own_p.astype(jnp.float32)[..., None] * own_v
    return mixed.reshape(rows, heads * HD)


WIDTH = 512
OUTWARD = ((0, 1), (1, 0), (2, 3), (3, 2))
ACROSS = ((0, 2), (2, 0), (1, 3), (3, 1))
MIDDLE = ((0, 1), (1, 0), (2, 4), (4, 2), (3, 5), (5, 3), (6, 7), (7, 6))
SWAP = ((0, 1), (1, 0))
f32 = jnp.float32
bf16 = jnp.bfloat16
ANY = pl.BlockSpec(memory_space=pl.ANY)
SMEM = pl.BlockSpec(memory_space=pltpu.SMEM)
VMEM = pl.BlockSpec(memory_space=pltpu.VMEM)


def outward(a):
    return lax.ppermute(a, "mix", OUTWARD)


def middle(a):
    return lax.ppermute(a, ("mix", "pair"), MIDDLE)


def swap(a, axis):
    return lax.ppermute(a, axis, SWAP)


def partial_products(k, rows, gate_rows, up_rows, after):
    count, depth = rows.shape
    units = gate_rows.shape[0]
    half = count // 2
    valid = min(WIDTH, units - k * WIDTH)
    step = 256
    steps = WIDTH // step

    def kernel(rows_ref, gate_ref, up_ref, *rest):
        out_ref, in_ref = rest[-2:]
        i = pl.program_id(0)
        for weight, offset in ((gate_ref, 0), (up_ref, WIDTH)):
            part = lax.dot_general(rows_ref[...], weight[...], (((1,), (1,)), ((), ())), preferred_element_type=f32)
            if valid < WIDTH:
                unit = lax.broadcasted_iota(jnp.int32, part.shape, 1) + i * step
                part = jnp.where(unit < valid, part, 0.0)
            part = part.astype(bf16)
            at = pl.ds(pl.multiple_of(offset + i * step, step), step)
            out_ref[:, at] = part[:half]
            in_ref[:, at] = part[half:]

    shape = jax.ShapeDtypeStruct((half, 2 * WIDTH), bf16)
    first = k * steps
    return pl.pallas_call(
        kernel,
        grid=(steps,),
        in_specs=[
            pl.BlockSpec((count, depth), lambda i: (0, 0)),
            pl.BlockSpec((step, depth), lambda i: (first + i, 0)),
            pl.BlockSpec((step, depth), lambda i: (first + i, 0)),
        ]
        + [ANY] * len(after),
        out_specs=[pl.BlockSpec((half, 2 * WIDTH), lambda i: (0, 0))] * 2,
        out_shape=[shape, shape],
        compiler_params=pltpu.CompilerParams(vmem_limit_bytes=24 << 20),
        cost_estimate=pl.CostEstimate(
            flops=4 * count * depth * WIDTH, bytes_accessed=4 * depth * WIDTH + 6 * count * WIDTH, transcendentals=0
        ),
        name="partial_products",
    )(rows, gate_rows, up_rows, *after)


def hop(outer, inv_in, t, count, got_e, got_m, part_out, part_in, after):
    half = inv_in.shape[0]

    def inside(k):
        return 0 <= k < count

    def sums_e(s):
        return inside(s) or inside(s - 2)

    def hid_e(s):
        return inside(s - 3) or inside(s - 5)

    two = 2 * WIDTH
    names = ["outer", "inv"]
    operands = [outer, inv_in]
    specs = [SMEM, VMEM]

    def add(name, value):
        names.append(name)
        operands.append(value)
        specs.append(VMEM)

    need_sum_in = inside(t - 2)
    if need_sum_in or hid_e(t) or inside(t):
        add("got_e", got_e)
    if got_m is not None and (inside(t - 1) or inside(t - 4)):
        add("got_m", got_m)
    if inside(t + 1):
        add("next_out", part_out[t + 1])
    if inside(t):
        add("out", part_out[t])
    if inside(t - 1):
        add("in1", part_in[t - 1])
    if inside(t - 2):
        add("in2", part_in[t - 2])
    operands += after
    specs += [ANY] * len(after)
    nxt = t + 1
    hid_at_e = two if sums_e(nxt) else 0
    hid_at_got_e = two if sums_e(t) else 0
    width_e = hid_at_e + (WIDTH if hid_e(nxt) else 0)
    hid_at_m = two if inside(t) else 0
    hid_at_got_m = two if inside(t - 1) else 0
    width_m = hid_at_m + (WIDTH if inside(t - 3) else 0)
    widths = [w for w in (width_e, width_m) if w]

    def kernel(*refs):
        r = dict(zip(names, refs))
        outs = list(refs[len(operands) :])
        to_e = outs.pop(0) if width_e else None
        to_m = outs.pop(0) if width_m else None

        @pl.when(r["outer"][0] != 0)
        def _():
            if inside(t + 1):
                to_e[:, :two] = r["next_out"][...]
            if inside(t - 2):
                inv = r["inv"][...]
                gate = (r["in2"][:, :WIDTH].astype(f32) + r["got_e"][:, :WIDTH].astype(f32)) * inv
                up = (r["in2"][:, WIDTH:].astype(f32) + r["got_e"][:, WIDTH:two].astype(f32)) * inv
                to_e[:, hid_at_e : hid_at_e + WIDTH] = (gate / (1.0 + jnp.exp(-gate)) * up).astype(bf16)

        @pl.when(r["outer"][0] == 0)
        def _():
            if inside(t - 1):
                to_e[:, :two] = (r["in1"][...].astype(f32) + r["got_m"][:, :two].astype(f32)).astype(bf16)
            if inside(t - 4):
                to_e[:, hid_at_e : hid_at_e + WIDTH] = r["got_m"][:, hid_at_got_m : hid_at_got_m + WIDTH]
            if inside(t):
                to_m[:, :two] = (r["out"][...].astype(f32) + r["got_e"][:, :two].astype(f32)).astype(bf16)
            if inside(t - 3):
                to_m[:, hid_at_m : hid_at_m + WIDTH] = r["got_e"][:, hid_at_got_e : hid_at_got_e + WIDTH]

    outs = pl.pallas_call(
        kernel,
        in_specs=specs,
        out_specs=[VMEM] * len(widths),
        out_shape=[jax.ShapeDtypeStruct((half, w), bf16) for w in widths],
        compiler_params=pltpu.CompilerParams(vmem_limit_bytes=24 << 20),
        cost_estimate=pl.CostEstimate(flops=8 * half * two, bytes_accessed=10 * half * two, transcendentals=half * WIDTH),
        name="hop",
    )(*operands)
    outs = list(outs)
    to_e = (outs.pop(0), hid_at_e) if width_e else None
    to_m = (outs.pop(0), hid_at_m) if width_m else None
    return to_e, to_m


def down_product(outer, total, first, chunks, w_down, final):
    units, columns = w_down.shape
    half = chunks[0][0][0].shape[0]
    n = len(chunks)
    valid = min(n * WIDTH, units - first * WIDTH)
    step = 512

    def kernel(outer_ref, *refs):
        hids = refs[: 4 * n]
        w_ref = refs[4 * n]
        total_ref = refs[4 * n + 1] if total is not None else None
        out_ref, hid = refs[-2:]

        @pl.when(pl.program_id(0) == 0)
        def _():
            for c in range(n):
                sent, got, from_m, late = hids[4 * c : 4 * c + 4]
                at = pl.ds(c * WIDTH, WIDTH)

                @pl.when(outer_ref[0] != 0)
                def _():
                    hid[:half, at] = late[...]
                    hid[half:, at] = sent[...]

                @pl.when(outer_ref[0] == 0)
                def _():
                    hid[:half, at] = from_m[...]
                    hid[half:, at] = got[...]

        weight = w_ref[...]
        if valid < n * WIDTH:
            unit = lax.broadcasted_iota(jnp.int32, weight.shape, 0)
            weight = jnp.where(unit < valid, weight.astype(f32), 0.0).astype(bf16)
        term = jnp.dot(hid[...], weight, preferred_element_type=f32)
        if total_ref is not None:
            term = term + total_ref[...]
        out_ref[...] = term.astype(out_ref.dtype)

    operands, specs = [outer], [SMEM]
    for chunk in chunks:
        for buffer, offset in chunk:
            operands.append(buffer)
            specs.append(pl.BlockSpec((half, WIDTH), functools.partial(lambda at, i: (0, at), offset // WIDTH)))
    operands.append(w_down)
    block = first // n
    specs.append(pl.BlockSpec((n * WIDTH, step), lambda i: (block, i)))
    if total is not None:
        operands.append(total)
        specs.append(pl.BlockSpec((2 * half, step), lambda i: (0, i)))
    return pl.pallas_call(
        kernel,
        grid=(columns // step,),
        in_specs=specs,
        out_specs=pl.BlockSpec((2 * half, step), lambda i: (0, i)),
        out_shape=jax.ShapeDtypeStruct((2 * half, columns), bf16 if final else f32),
        scratch_shapes=[pltpu.VMEM((2 * half, n * WIDTH), bf16)],
        compiler_params=pltpu.CompilerParams(vmem_limit_bytes=24 << 20),
        cost_estimate=pl.CostEstimate(
            flops=4 * half * n * WIDTH * columns,
            bytes_accessed=2 * n * WIDTH * columns + 16 * half * columns,
            transcendentals=0,
        ),
        name="down_product",
    )(*operands)


def mlp_line(scaled, rows_rms, w_gate, w_up, w_down):
    place = lax.axis_index("mix")
    left = place < 2
    outer = ((place == 0) | (place == 3)).astype(jnp.int32).reshape(1)

    across = swap(scaled, "ffn")
    beside = swap(scaled, "pair")
    diagonal = swap(across, "pair")
    here = jnp.concatenate([scaled, across])
    there = jnp.concatenate([beside, diagonal])
    rows = jnp.concatenate([jnp.where(left, here, there), jnp.where(left, there, here)])
    half = here.shape[0]

    inv = jnp.concatenate([rows_rms, swap(rows_rms, "ffn")])
    inv_in = jnp.where(left, swap(inv, "pair"), inv)

    gate_rows = pltpu.with_memory_space_constraint(w_gate.T, pltpu.HBM)
    up_rows = pltpu.with_memory_space_constraint(w_up.T, pltpu.HBM)
    w_down = pltpu.with_memory_space_constraint(w_down, pltpu.HBM)
    chunks = -(-gate_rows.shape[0] // WIDTH)
    counts = (-(-chunks // 2), chunks // 2)
    part_out, part_in = ({}, {}), ({}, {})
    sent, got = {}, {}

    def products(k, after):
        if k < chunks:
            a, b = partial_products(k, rows, gate_rows, up_rows, after)
            part_out[k % 2][k // 2], part_in[k % 2][k // 2] = a, b
            return [a]
        return after

    def send(s, t, to_e, to_m):
        sent["e", s, t], sent["m", s, t] = to_e, to_m
        got["e", s, t] = (outward(to_e[0]), to_e[1]) if to_e else None
        got["m", s, t] = (middle(to_m[0]), to_m[1]) if to_m else None

    def hidden_of(k):
        s, j = k % 2, k // 2
        return [sent["e", s, j + 3], got["e", s, j + 3], got["m", s, j + 4], got["e", s, j + 5]]

    after = products(0, [])
    send(0, 0, (part_out[0][0], 2 * WIDTH), None)
    after = products(1, after)
    send(1, 0, (part_out[1][0], 2 * WIDTH), None)
    after = products(2, after)
    total = None
    for t in range(counts[0] + 5):
        for s in (0, 1):
            count = counts[s]
            if t < count + 4:
                got_e, got_m = got["e", s, t], got["m", s, t]
                to_e, to_m = hop(
                    outer,
                    inv_in,
                    t,
                    count,
                    got_e and got_e[0],
                    got_m and got_m[0],
                    part_out[s],
                    part_in[s],
                    after,
                )
                send(s, t + 1, to_e, to_m)
                after = [(to_e or to_m)[0]]
            after = products(2 * t + s + 3, after)
            first = 2 * (t - 5)
            if first >= 0 and ((s == 1 and first + 1 < chunks) or (s == 0 and first + 1 == chunks)):
                pair = [hidden_of(k) for k in range(first, min(first + 2, chunks))]
                total = down_product(outer, total, first, pair, w_down, first + 2 >= chunks)
                after = [total]
    far, near = total[:half], total[half:]
    for_here = jnp.where(left, far, near)
    for_there = jnp.where(left, near, far)
    chip = for_here.astype(f32) + swap(for_there, "pair").astype(f32)
    block = half // 2
    return chip[:block] + swap(chip[block:].astype(bf16), "ffn").astype(f32)


def mlp_sums(normed, w_gate, w_up, w_down):
    gathered = lax.all_gather(normed, ("ffn", "pair"), axis=0, tiled=True)
    parts = []
    for weight in (w_gate, w_up):
        part = jnp.dot(gathered, weight, preferred_element_type=jnp.float32).astype(jnp.bfloat16)
        parts.append(lax.psum_scatter(part, "mix", scatter_dimension=0, tiled=True).astype(jnp.float32))
    hidden = (jax.nn.silu(parts[0]) * parts[1]).astype(jnp.bfloat16)
    hidden = lax.all_gather(hidden, "mix", axis=0, tiled=True)
    partial_value = jnp.dot(hidden, w_down, preferred_element_type=jnp.float32)
    return lax.psum_scatter(
        partial_value.astype(jnp.bfloat16), ("ffn", "pair"), scatter_dimension=0, tiled=True
    ).astype(jnp.float32)


def per_device(
    on_line,
    query,
    new_key,
    new_value,
    key_cache,
    value_cache,
    lengths,
    counts,
    residual,
    norm_gain,
    w_gate,
    w_up,
    w_down,
):
    mixed = attend(query, new_key, new_value, key_cache, value_cache, lengths)
    x = residual.astype(jnp.float32) + mixed
    gain = norm_gain.astype(jnp.float32)
    squares = jnp.sum(x * x, axis=1, keepdims=True)
    if on_line:
        squares = squares + outward(squares)
        squares = squares + lax.ppermute(squares, "mix", ACROSS)
        inv = lax.rsqrt(squares / D + eps)
        mlp = mlp_line((x * gain).astype(jnp.bfloat16), inv, w_gate, w_up, w_down)
    else:
        inv = lax.rsqrt(lax.psum(squares, "mix") / D + eps)
        mlp = mlp_sums((x * inv * gain).astype(jnp.bfloat16), w_gate, w_up, w_down)
    slots = jnp.arange(x.shape[0], dtype=jnp.int32)
    live = slots < counts[0]
    return jnp.where(live[:, None], x + mlp, jnp.zeros_like(x)).astype(jnp.bfloat16)


def solution(mesh):
    sizes = mesh.shape
    on_line = sizes["mix"] == 4 and sizes["ffn"] == 2 and sizes["pair"] == 2
    placed = (
        P(("grp", "ffn", "pair"), "mix"),
        P(("grp", "ffn", "pair"), "mix"),
        P(("grp", "ffn", "pair"), "mix"),
        P(("grp", "ffn", "pair"), None, "mix"),
        P(("grp", "ffn", "pair"), None, "mix"),
        P(("grp", "ffn", "pair")),
        P(("grp", "ffn", "pair")),
        P(("grp", "ffn", "pair"), "mix"),
        P("mix"),
        P("mix", ("ffn", "pair")),
        P("mix", ("ffn", "pair")),
        P(("ffn", "pair"), "mix"),
    )
    return jax.shard_map(
        functools.partial(per_device, on_line),
        mesh=mesh,
        in_specs=placed,
        out_specs=P(("grp", "ffn", "pair"), "mix"),
        check_vma=False,
    )
```

```python
import functools

import jax
import jax.numpy as jnp
from jax import lax
from jax.experimental import pallas as pl
from jax.experimental.pallas import tpu as pltpu
from jax.sharding import PartitionSpec as P

D = 8192
HD = 128


eps = 1e-05


def attend(query, new_key, new_value, key_cache, value_cache, lengths):
    rows = query.shape[0]
    heads = query.shape[1] // HD
    cache_len = key_cache.shape[1]
    scale = 1.0 / HD**0.5
    q_heads = query.reshape(rows, heads, HD)
    k_all = key_cache.reshape(rows, cache_len, heads, HD)
    v_all = value_cache.reshape(rows, cache_len, heads, HD)
    scores = jnp.einsum("chd,cphd->chp", q_heads, k_all, preferred_element_type=jnp.float32) * scale
    own = (
        jnp.einsum(
            "chd,chd->ch",
            q_heads,
            new_key.reshape(rows, heads, HD),
            preferred_element_type=jnp.float32,
        )
        * scale
    )
    valid = jnp.arange(cache_len, dtype=jnp.int32)[None, :] < lengths[:, None]
    scores = jnp.where(valid[:, None, :], scores, -jnp.inf)
    top = jnp.maximum(jnp.max(scores, axis=-1), own)
    weights = jnp.exp(scores - top[..., None])
    own_w = jnp.exp(own - top)
    total = jnp.sum(weights, axis=-1) + own_w
    probs = (weights / total[..., None]).astype(jnp.bfloat16)
    own_p = (own_w / total).astype(jnp.bfloat16)
    mixed = jnp.einsum("chp,cphd->chd", probs, v_all, preferred_element_type=jnp.float32)
    own_v = new_value.reshape(rows, heads, HD).astype(jnp.float32)
    mixed = mixed + own_p.astype(jnp.float32)[..., None] * own_v
    return mixed.reshape(rows, heads * HD)


WIDTH = 512
LANES = 128
TWO = 2 * WIDTH
SCALE = 4
OUTWARD = ((0, 1), (1, 0), (2, 3), (3, 2))
ACROSS = ((0, 2), (2, 0), (1, 3), (3, 1))
MIDDLE = ((0, 1), (1, 0), (2, 4), (4, 2), (3, 5), (5, 3), (6, 7), (7, 6))
SWAP = ((0, 1), (1, 0))
f32 = jnp.float32
bf16 = jnp.bfloat16
ANY = pl.BlockSpec(memory_space=pl.ANY)
SMEM = pl.BlockSpec(memory_space=pltpu.SMEM)
VMEM = pl.BlockSpec(memory_space=pltpu.VMEM)


def cost(flops, moved):
    return pl.CostEstimate(flops=int(flops * SCALE), bytes_accessed=int(moved * SCALE), transcendentals=0)


def outward(a):
    return lax.ppermute(a, "mix", OUTWARD)


def middle(a):
    return lax.ppermute(a, ("mix", "pair"), MIDDLE)


def swap(a, axis):
    return lax.ppermute(a, axis, SWAP)


def chunk_columns(k):
    return TWO + (LANES if k == 0 else 0)


def in_three(total, shape):
    lane = lax.broadcasted_iota(jnp.int32, shape, 1)
    high = total.astype(bf16).astype(f32)
    middle_part = (total - high).astype(bf16).astype(f32)
    low = total - high - middle_part
    three = jnp.where(lane == 0, high, jnp.where(lane == 1, middle_part, jnp.where(lane == 2, low, 0.0)))
    return three.astype(bf16)


def add_in_three(a, b):
    lane = lax.broadcasted_iota(jnp.int32, a.shape, 1)
    total = jnp.sum(jnp.where(lane < 3, a.astype(f32) + b.astype(f32), 0.0), axis=1, keepdims=True)
    return total, in_three(total, a.shape)


def attend_rows(query, new_key, new_value, key_cache, value_cache, lengths, residual, norm_gain):
    rows, features = query.shape
    heads = features // HD
    cache_len = key_cache.shape[1]
    block = 16
    tall, wide = heads * block, block * cache_len
    scale = 1.0 / HD**0.5
    held = functools.partial(pltpu.with_memory_space_constraint, memory_space=pltpu.HBM)

    def kernel(length_ref, q_ref, nk_ref, nv_ref, k_ref, v_ref, res_ref, gain_ref, x_ref, scaled_ref, sparse):
        @pl.when(pl.program_id(0) == 0)
        def _():
            sparse[...] = jnp.zeros_like(sparse)

        for h in range(heads):
            sparse[h * block : (h + 1) * block, h * HD : (h + 1) * HD] = q_ref[:, h * HD : (h + 1) * HD]
        q_rows = sparse[...]
        over = (((1,), (1,)), ((), ()))
        keys = k_ref[...].reshape(wide, features)
        scores = lax.dot_general(q_rows, keys, over, preferred_element_type=f32) * scale
        own = lax.dot_general(q_rows, nk_ref[...], over, preferred_element_type=f32) * scale
        mine = lax.broadcasted_iota(jnp.int32, own.shape, 0) % block == lax.broadcasted_iota(jnp.int32, own.shape, 1)
        own = jnp.sum(jnp.where(mine, own, 0.0), axis=1, keepdims=True)
        column = lax.broadcasted_iota(jnp.int32, scores.shape, 1)
        owner = lax.broadcasted_iota(jnp.int32, scores.shape, 0) % block
        offset = column - owner * cache_len
        candidate = lax.broadcasted_iota(jnp.int32, (tall, 1), 0) % block
        span = jnp.zeros((tall, 1), jnp.int32)
        for c in range(block):
            span = jnp.where(candidate == c, length_ref[pl.program_id(0) * block + c], span)
        valid = (offset >= 0) & (offset < span)
        scores = jnp.where(valid, scores, -jnp.inf)
        top = jnp.maximum(jnp.max(scores, axis=1, keepdims=True), own)
        weights = jnp.exp(scores - top)
        own_w = jnp.exp(own - top)
        total = jnp.sum(weights, axis=1, keepdims=True) + own_w
        probs = (weights / total).astype(bf16)
        own_p = (own_w / total).astype(bf16).astype(f32)
        mixed = jnp.dot(probs, v_ref[...].reshape(wide, features), preferred_element_type=f32)
        squares = jnp.zeros((block, HD), f32)
        for h in range(heads):
            at, rows_at = slice(h * HD, (h + 1) * HD), slice(h * block, (h + 1) * block)
            x = res_ref[:, at].astype(f32) + mixed[rows_at, at] + own_p[rows_at] * nv_ref[:, at].astype(f32)
            x_ref[:, at] = x
            scaled_ref[:, at] = (x * gain_ref[:, at].astype(f32)).astype(bf16)
            squares = squares + x * x
        scaled_ref[:, features:] = in_three(jnp.sum(squares, axis=1, keepdims=True), (block, LANES))

    flat = pl.BlockSpec((block, features), lambda i: (i, 0))
    cache = pl.BlockSpec((block, cache_len, features), lambda i: (i, 0, 0))
    return pl.pallas_call(
        kernel,
        grid=(rows // block,),
        in_specs=[
            SMEM,
            flat,
            flat,
            flat,
            cache,
            cache,
            flat,
            pl.BlockSpec((1, features), lambda i: (0, 0)),
        ],
        out_specs=[flat, pl.BlockSpec((block, features + LANES), lambda i: (i, 0))],
        out_shape=[
            jax.ShapeDtypeStruct((rows, features), f32),
            jax.ShapeDtypeStruct((rows, features + LANES), bf16),
        ],
        scratch_shapes=[pltpu.VMEM((tall, features), bf16)],
        compiler_params=pltpu.CompilerParams(vmem_limit_bytes=40 << 20),
        cost_estimate=pl.CostEstimate(
            flops=4 * rows // block * tall * wide * features,
            bytes_accessed=4 * rows * cache_len * features,
            transcendentals=rows // block * tall * wide,
        ),
        name="attend_rows",
    )(
        lengths,
        held(query),
        held(new_key),
        held(new_value),
        held(key_cache),
        held(value_cache),
        held(residual),
        norm_gain.reshape(1, -1),
    )


def partial_products(k, rows, gate_rows, up_rows, after):
    count = rows.shape[0]
    units = gate_rows.shape[0]
    half = count // 2
    valid = min(WIDTH, units - k * WIDTH)
    step = 256
    steps = WIDTH // step
    depth = gate_rows.shape[1]
    columns = chunk_columns(k)

    def kernel(rows_ref, gate_ref, up_ref, *rest):
        out_ref, in_ref = rest[-2:]
        i = pl.program_id(0)
        if columns > TWO:
            out_ref[:, TWO:] = rest[0][:half]
            in_ref[:, TWO:] = rest[0][half:]
        for weight, offset in ((gate_ref, 0), (up_ref, WIDTH)):
            part = lax.dot_general(rows_ref[...], weight[...], (((1,), (1,)), ((), ())), preferred_element_type=f32)
            if valid < WIDTH:
                unit = lax.broadcasted_iota(jnp.int32, part.shape, 1) + i * step
                part = jnp.where(unit < valid, part, 0.0)
            part = part.astype(bf16)
            at = pl.ds(pl.multiple_of(offset + i * step, step), step)
            out_ref[:, at] = part[:half]
            in_ref[:, at] = part[half:]

    shape = jax.ShapeDtypeStruct((half, columns), bf16)
    first = k * steps
    return pl.pallas_call(
        kernel,
        grid=(steps,),
        in_specs=[
            pl.BlockSpec((count, depth), lambda i: (0, 0)),
            pl.BlockSpec((step, depth), lambda i: (first + i, 0)),
            pl.BlockSpec((step, depth), lambda i: (first + i, 0)),
        ]
        + ([pl.BlockSpec((count, LANES), lambda i: (0, depth // LANES))] if columns > TWO else [])
        + [ANY] * len(after),
        out_specs=[pl.BlockSpec((half, columns), lambda i: (0, 0))] * 2,
        out_shape=[shape, shape],
        compiler_params=pltpu.CompilerParams(vmem_limit_bytes=24 << 20),
        cost_estimate=cost(4 * count * depth * WIDTH, 4 * depth * WIDTH + 6 * count * WIDTH),
        name="partial_products",
    )(rows, gate_rows, up_rows, *([rows] if columns > TWO else []), *after)


def hop(outer, inv_in, s, t, count, got_e, got_m, part_out, part_in, after):
    half = part_out[0].shape[0]

    def inside(j):
        return 0 <= j < count

    def columns(*js):
        return max([chunk_columns(2 * j + s) for j in js if inside(j)], default=0)

    def hid_e(step):
        return inside(step - 3) or inside(step - 5)

    names, operands, specs = ["outer"], [outer], [SMEM]

    def add(name, value):
        names.append(name)
        operands.append(value)
        specs.append(VMEM)

    if columns(t, t - 2) or hid_e(t):
        add("got_e", got_e)
    if got_m is not None and (inside(t - 1) or inside(t - 4)):
        add("got_m", got_m)
    if inside(t + 1):
        add("next_out", part_out[t + 1])
    if inside(t):
        add("out", part_out[t])
    if inside(t - 1):
        add("in1", part_in[t - 1])
    starts_inv = inside(t - 2) and columns(t - 2) > TWO
    if inside(t - 2):
        add("in2", part_in[t - 2])
        if not starts_inv:
            add("inv", inv_in)
    operands += after
    specs += [ANY] * len(after)
    nxt = t + 1
    hid_at_e = columns(nxt, nxt - 2)
    hid_at_got_e = columns(t, t - 2)
    width_e = hid_at_e + (WIDTH if hid_e(nxt) else 0)
    hid_at_m = columns(t)
    hid_at_got_m = columns(t - 1)
    width_m = hid_at_m + (WIDTH if inside(t - 3) else 0)
    widths = [w for w in (width_e, width_m) if w]

    def kernel(*refs):
        r = dict(zip(names, refs))
        outs = list(refs[len(operands) :])
        to_e = outs.pop(0) if width_e else None
        to_m = outs.pop(0) if width_m else None

        def both(own, received, to, j):
            to[:, :TWO] = (own[:, :TWO].astype(f32) + received[:, :TWO].astype(f32)).astype(bf16)
            if columns(j) > TWO:
                to[:, TWO : columns(j)] = add_in_three(own[:, TWO:], received[:, TWO : columns(j)])[1]

        @pl.when(r["outer"][0] != 0)
        def _():
            if inside(t + 1):
                to_e[:, :TWO] = r["next_out"][:, :TWO]
            if inside(t - 2):
                if starts_inv:
                    squares, _ = add_in_three(r["in2"][:, TWO:], r["got_e"][:, TWO : TWO + LANES])
                    inv = lax.rsqrt(squares / D + eps)
                    outs[0][...] = inv
                else:
                    inv = r["inv"][...]
                gate = (r["in2"][:, :WIDTH].astype(f32) + r["got_e"][:, :WIDTH].astype(f32)) * inv
                up = (r["in2"][:, WIDTH:TWO].astype(f32) + r["got_e"][:, WIDTH:TWO].astype(f32)) * inv
                to_e[:, hid_at_e : hid_at_e + WIDTH] = (gate / (1.0 + jnp.exp(-gate)) * up).astype(bf16)

        @pl.when(r["outer"][0] == 0)
        def _():
            if inside(t - 1):
                both(r["in1"], r["got_m"], to_e, t - 1)
            if inside(t - 4):
                to_e[:, hid_at_e : hid_at_e + WIDTH] = r["got_m"][:, hid_at_got_m : hid_at_got_m + WIDTH]
            if inside(t):
                both(r["out"], r["got_e"], to_m, t)
            if inside(t - 3):
                to_m[:, hid_at_m : hid_at_m + WIDTH] = r["got_e"][:, hid_at_got_e : hid_at_got_e + WIDTH]
            if starts_inv:
                outs[0][...] = jnp.zeros(outs[0].shape, f32)

    shapes = [jax.ShapeDtypeStruct((half, w), bf16) for w in widths]
    if starts_inv:
        shapes.append(jax.ShapeDtypeStruct((half, 1), f32))
    outs = pl.pallas_call(
        kernel,
        in_specs=specs,
        out_specs=[VMEM] * len(shapes),
        out_shape=shapes,
        compiler_params=pltpu.CompilerParams(vmem_limit_bytes=24 << 20),
        cost_estimate=cost(8 * half * TWO, 10 * half * TWO),
        name="hop",
    )(*operands)
    outs = list(outs)
    to_e = (outs.pop(0), hid_at_e) if width_e else None
    to_m = (outs.pop(0), hid_at_m) if width_m else None
    return to_e, to_m, outs[0] if outs else inv_in


def down_product(outer, total, first, chunks, w_down, final):
    units, columns = w_down.shape
    half = chunks[0][0][0].shape[0]
    n = len(chunks)
    valid = min(n * WIDTH, units - first * WIDTH)
    step = 512

    def kernel(outer_ref, *refs):
        hids = refs[: 4 * n]
        w_ref = refs[4 * n]
        total_ref = refs[4 * n + 1] if total is not None else None
        out_ref, hid = refs[-2:]

        @pl.when(pl.program_id(0) == 0)
        def _():
            for c in range(n):
                sent, got, from_m, late = hids[4 * c : 4 * c + 4]
                at = pl.ds(c * WIDTH, WIDTH)

                @pl.when(outer_ref[0] != 0)
                def _():
                    hid[:half, at] = late[...]
                    hid[half:, at] = sent[...]

                @pl.when(outer_ref[0] == 0)
                def _():
                    hid[:half, at] = from_m[...]
                    hid[half:, at] = got[...]

        weight = w_ref[...]
        if valid < n * WIDTH:
            unit = lax.broadcasted_iota(jnp.int32, weight.shape, 0)
            weight = jnp.where(unit < valid, weight.astype(f32), 0.0).astype(bf16)
        term = jnp.dot(hid[...], weight, preferred_element_type=f32)
        if total_ref is not None:
            term = term + total_ref[...]
        out_ref[...] = term.astype(out_ref.dtype)

    operands, specs = [outer], [SMEM]
    for chunk in chunks:
        for buffer, offset in chunk:
            operands.append(buffer)
            specs.append(pl.BlockSpec((half, WIDTH), functools.partial(lambda at, i: (0, at), offset // WIDTH)))
    operands.append(w_down)
    block = first // n
    specs.append(pl.BlockSpec((n * WIDTH, step), lambda i: (block, i)))
    if total is not None:
        operands.append(total)
        specs.append(pl.BlockSpec((2 * half, step), lambda i: (0, i)))
    return pl.pallas_call(
        kernel,
        grid=(columns // step,),
        in_specs=specs,
        out_specs=pl.BlockSpec((2 * half, step), lambda i: (0, i)),
        out_shape=jax.ShapeDtypeStruct((2 * half, columns), bf16 if final else f32),
        scratch_shapes=[pltpu.VMEM((2 * half, n * WIDTH), bf16)],
        compiler_params=pltpu.CompilerParams(vmem_limit_bytes=24 << 20),
        cost_estimate=cost(4 * half * n * WIDTH * columns, 2 * n * WIDTH * columns + 16 * half * columns),
        name="down_product",
    )(*operands)


def mlp_line(scaled, w_gate, w_up, w_down):
    place = lax.axis_index("mix")
    left = place < 2
    outer = ((place == 0) | (place == 3)).astype(jnp.int32).reshape(1)

    across = swap(scaled, "ffn")
    beside = swap(scaled, "pair")
    diagonal = swap(across, "pair")
    here = jnp.concatenate([scaled, across])
    there = jnp.concatenate([beside, diagonal])
    rows = jnp.concatenate([jnp.where(left, here, there), jnp.where(left, there, here)])
    half = here.shape[0]

    gate_rows = pltpu.with_memory_space_constraint(w_gate.T, pltpu.HBM)
    up_rows = pltpu.with_memory_space_constraint(w_up.T, pltpu.HBM)
    w_down = pltpu.with_memory_space_constraint(w_down, pltpu.HBM)
    chunks = -(-gate_rows.shape[0] // WIDTH)
    counts = (-(-chunks // 2), chunks // 2)
    part_out, part_in = ({}, {}), ({}, {})
    sent, got = {}, {}

    def products(k, after):
        if k < chunks:
            a, b = partial_products(k, rows, gate_rows, up_rows, after)
            part_out[k % 2][k // 2], part_in[k % 2][k // 2] = a, b
            return [a]
        return after

    def send(s, t, to_e, to_m):
        sent["e", s, t], sent["m", s, t] = to_e, to_m
        got["e", s, t] = (outward(to_e[0]), to_e[1]) if to_e else None
        got["m", s, t] = (middle(to_m[0]), to_m[1]) if to_m else None

    def hidden_of(k):
        s, j = k % 2, k // 2
        return [sent["e", s, j + 3], got["e", s, j + 3], got["m", s, j + 4], got["e", s, j + 5]]

    after = products(0, [])
    send(0, 0, (part_out[0][0], TWO), None)
    after = products(1, after)
    send(1, 0, (part_out[1][0], TWO), None)
    after = products(2, after)
    total, inv_in = None, None
    for t in range(counts[0] + 5):
        for s in (0, 1):
            count = counts[s]
            if t < count + 4:
                got_e, got_m = got["e", s, t], got["m", s, t]
                to_e, to_m, inv_in = hop(
                    outer,
                    inv_in,
                    s,
                    t,
                    count,
                    got_e and got_e[0],
                    got_m and got_m[0],
                    part_out[s],
                    part_in[s],
                    after,
                )
                send(s, t + 1, to_e, to_m)
                after = [(to_e or to_m)[0]]
            after = products(2 * t + s + 3, after)
            first = 2 * (t - 5)
            if first >= 0 and ((s == 1 and first + 1 < chunks) or (s == 0 and first + 1 == chunks)):
                pair = [hidden_of(k) for k in range(first, min(first + 2, chunks))]
                total = down_product(outer, total, first, pair, w_down, first + 2 >= chunks)
                after = [total]
    far, near = total[:half], total[half:]
    for_here = jnp.where(left, far, near)
    for_there = jnp.where(left, near, far)
    chip = for_here.astype(f32) + swap(for_there, "pair").astype(f32)
    block = half // 2
    return chip[:block] + swap(chip[block:].astype(bf16), "ffn").astype(f32)


def mlp_sums(normed, w_gate, w_up, w_down):
    gathered = lax.all_gather(normed, ("ffn", "pair"), axis=0, tiled=True)
    parts = []
    for weight in (w_gate, w_up):
        part = jnp.dot(gathered, weight, preferred_element_type=jnp.float32).astype(jnp.bfloat16)
        parts.append(lax.psum_scatter(part, "mix", scatter_dimension=0, tiled=True).astype(jnp.float32))
    hidden = (jax.nn.silu(parts[0]) * parts[1]).astype(jnp.bfloat16)
    hidden = lax.all_gather(hidden, "mix", axis=0, tiled=True)
    partial_value = jnp.dot(hidden, w_down, preferred_element_type=jnp.float32)
    return lax.psum_scatter(
        partial_value.astype(jnp.bfloat16), ("ffn", "pair"), scatter_dimension=0, tiled=True
    ).astype(jnp.float32)


def per_device(
    on_line,
    query,
    new_key,
    new_value,
    key_cache,
    value_cache,
    lengths,
    counts,
    residual,
    norm_gain,
    w_gate,
    w_up,
    w_down,
):
    if on_line:
        x, scaled = attend_rows(
            query, new_key, new_value, key_cache, value_cache, lengths, residual, norm_gain
        )
        mlp = mlp_line(scaled, w_gate, w_up, w_down)
    else:
        x = residual.astype(f32) + attend(query, new_key, new_value, key_cache, value_cache, lengths)
        inv = lax.rsqrt(lax.psum(jnp.sum(x * x, axis=1, keepdims=True), "mix") / D + eps)
        normed = (x * inv * norm_gain.astype(f32)).astype(bf16)
        mlp = mlp_sums(normed, w_gate, w_up, w_down)
    slots = jnp.arange(x.shape[0], dtype=jnp.int32)
    live = slots < counts[0]
    return jnp.where(live[:, None], x + mlp, jnp.zeros_like(x)).astype(jnp.bfloat16)


def solution(mesh):
    sizes = mesh.shape
    on_line = sizes["mix"] == 4 and sizes["ffn"] == 2 and sizes["pair"] == 2
    placed = (
        P(("grp", "ffn", "pair"), "mix"),
        P(("grp", "ffn", "pair"), "mix"),
        P(("grp", "ffn", "pair"), "mix"),
        P(("grp", "ffn", "pair"), None, "mix"),
        P(("grp", "ffn", "pair"), None, "mix"),
        P(("grp", "ffn", "pair")),
        P(("grp", "ffn", "pair")),
        P(("grp", "ffn", "pair"), "mix"),
        P("mix"),
        P("mix", ("ffn", "pair")),
        P("mix", ("ffn", "pair")),
        P(("ffn", "pair"), "mix"),
    )
    return jax.shard_map(
        functools.partial(per_device, on_line),
        mesh=mesh,
        in_specs=placed,
        out_specs=P(("grp", "ffn", "pair"), "mix"),
        check_vma=False,
    )
```

```python
import functools

import jax
import jax.numpy as jnp
from jax import lax
from jax.experimental import pallas as pl
from jax.experimental.pallas import tpu as pltpu
from jax.sharding import PartitionSpec as P

D = 8192
HD = 128


eps = 1e-05


def attend(query, new_key, new_value, key_cache, value_cache, lengths):
    rows = query.shape[0]
    heads = query.shape[1] // HD
    cache_len = key_cache.shape[1]
    scale = 1.0 / HD**0.5
    q_heads = query.reshape(rows, heads, HD)
    k_all = key_cache.reshape(rows, cache_len, heads, HD)
    v_all = value_cache.reshape(rows, cache_len, heads, HD)
    scores = jnp.einsum("chd,cphd->chp", q_heads, k_all, preferred_element_type=jnp.float32) * scale
    own = (
        jnp.einsum(
            "chd,chd->ch",
            q_heads,
            new_key.reshape(rows, heads, HD),
            preferred_element_type=jnp.float32,
        )
        * scale
    )
    valid = jnp.arange(cache_len, dtype=jnp.int32)[None, :] < lengths[:, None]
    scores = jnp.where(valid[:, None, :], scores, -jnp.inf)
    top = jnp.maximum(jnp.max(scores, axis=-1), own)
    weights = jnp.exp(scores - top[..., None])
    own_w = jnp.exp(own - top)
    total = jnp.sum(weights, axis=-1) + own_w
    probs = (weights / total[..., None]).astype(jnp.bfloat16)
    own_p = (own_w / total).astype(jnp.bfloat16)
    mixed = jnp.einsum("chp,cphd->chd", probs, v_all, preferred_element_type=jnp.float32)
    own_v = new_value.reshape(rows, heads, HD).astype(jnp.float32)
    mixed = mixed + own_p.astype(jnp.float32)[..., None] * own_v
    return mixed.reshape(rows, heads * HD)


WIDTH = 512
LANES = 128
TWO = 2 * WIDTH
SCALE = 4
OUTWARD = ((0, 1), (1, 0), (2, 3), (3, 2))
ACROSS = ((0, 2), (2, 0), (1, 3), (3, 1))
MIDDLE = ((0, 1), (1, 0), (2, 4), (4, 2), (3, 5), (5, 3), (6, 7), (7, 6))
SWAP = ((0, 1), (1, 0))
f32 = jnp.float32
bf16 = jnp.bfloat16
ANY = pl.BlockSpec(memory_space=pl.ANY)
SMEM = pl.BlockSpec(memory_space=pltpu.SMEM)
VMEM = pl.BlockSpec(memory_space=pltpu.VMEM)


def cost(flops, moved):
    return pl.CostEstimate(flops=int(flops * SCALE), bytes_accessed=int(moved * SCALE), transcendentals=0)


def outward(a):
    return lax.ppermute(a, "mix", OUTWARD)


def middle(a):
    return lax.ppermute(a, ("mix", "pair"), MIDDLE)


def swap(a, axis):
    return lax.ppermute(a, axis, SWAP)


def chunk_columns(k):
    return TWO + (LANES if k == 0 else 0)


def in_three(total, shape):
    lane = lax.broadcasted_iota(jnp.int32, shape, 1)
    high = total.astype(bf16).astype(f32)
    middle_part = (total - high).astype(bf16).astype(f32)
    low = total - high - middle_part
    three = jnp.where(lane == 0, high, jnp.where(lane == 1, middle_part, jnp.where(lane == 2, low, 0.0)))
    return three.astype(bf16)


def add_in_three(a, b):
    lane = lax.broadcasted_iota(jnp.int32, a.shape, 1)
    total = jnp.sum(jnp.where(lane < 3, a.astype(f32) + b.astype(f32), 0.0), axis=1, keepdims=True)
    return total, in_three(total, a.shape)


def attend_rows(query, new_key, new_value, key_cache, value_cache, lengths, residual, norm_gain):
    rows, features = query.shape
    heads = features // HD
    cache_len = key_cache.shape[1]
    block = 16
    tall, wide = heads * block, block * cache_len
    scale = 1.0 / HD**0.5
    held = functools.partial(pltpu.with_memory_space_constraint, memory_space=pltpu.HBM)

    def kernel(length_ref, q_ref, nk_ref, nv_ref, k_ref, v_ref, res_ref, gain_ref, x_ref, scaled_ref, sparse):
        @pl.when(pl.program_id(0) == 0)
        def _():
            sparse[...] = jnp.zeros_like(sparse)

        for h in range(heads):
            sparse[h * block : (h + 1) * block, h * HD : (h + 1) * HD] = q_ref[:, h * HD : (h + 1) * HD]
        q_rows = sparse[...]
        over = (((1,), (1,)), ((), ()))
        keys = k_ref[...].reshape(wide, features)
        scores = lax.dot_general(q_rows, keys, over, preferred_element_type=f32) * scale
        own = lax.dot_general(q_rows, nk_ref[...], over, preferred_element_type=f32) * scale
        mine = lax.broadcasted_iota(jnp.int32, own.shape, 0) % block == lax.broadcasted_iota(jnp.int32, own.shape, 1)
        own = jnp.sum(jnp.where(mine, own, 0.0), axis=1, keepdims=True)
        column = lax.broadcasted_iota(jnp.int32, scores.shape, 1)
        owner = lax.broadcasted_iota(jnp.int32, scores.shape, 0) % block
        offset = column - owner * cache_len
        candidate = lax.broadcasted_iota(jnp.int32, (tall, 1), 0) % block
        span = jnp.zeros((tall, 1), jnp.int32)
        for c in range(block):
            span = jnp.where(candidate == c, length_ref[pl.program_id(0) * block + c], span)
        valid = (offset >= 0) & (offset < span)
        scores = jnp.where(valid, scores, -jnp.inf)
        top = jnp.maximum(jnp.max(scores, axis=1, keepdims=True), own)
        weights = jnp.exp(scores - top)
        own_w = jnp.exp(own - top)
        total = jnp.sum(weights, axis=1, keepdims=True) + own_w
        probs = (weights / total).astype(bf16)
        own_p = (own_w / total).astype(bf16).astype(f32)
        mixed = jnp.dot(probs, v_ref[...].reshape(wide, features), preferred_element_type=f32)
        squares = jnp.zeros((block, HD), f32)
        for h in range(heads):
            at, rows_at = slice(h * HD, (h + 1) * HD), slice(h * block, (h + 1) * block)
            x = res_ref[:, at].astype(f32) + mixed[rows_at, at] + own_p[rows_at] * nv_ref[:, at].astype(f32)
            x_ref[:, at] = x
            scaled_ref[:, at] = (x * gain_ref[:, at].astype(f32)).astype(bf16)
            squares = squares + x * x
        scaled_ref[:, features:] = in_three(jnp.sum(squares, axis=1, keepdims=True), (block, LANES))

    flat = pl.BlockSpec((block, features), lambda i: (i, 0))
    cache = pl.BlockSpec((block, cache_len, features), lambda i: (i, 0, 0))
    return pl.pallas_call(
        kernel,
        grid=(rows // block,),
        in_specs=[
            SMEM,
            flat,
            flat,
            flat,
            cache,
            cache,
            flat,
            pl.BlockSpec((1, features), lambda i: (0, 0)),
        ],
        out_specs=[flat, pl.BlockSpec((block, features + LANES), lambda i: (i, 0))],
        out_shape=[
            jax.ShapeDtypeStruct((rows, features), f32),
            jax.ShapeDtypeStruct((rows, features + LANES), bf16),
        ],
        scratch_shapes=[pltpu.VMEM((tall, features), bf16)],
        compiler_params=pltpu.CompilerParams(vmem_limit_bytes=40 << 20),
        cost_estimate=pl.CostEstimate(
            flops=4 * rows // block * tall * wide * features,
            bytes_accessed=4 * rows * cache_len * features,
            transcendentals=rows // block * tall * wide,
        ),
        name="attend_rows",
    )(
        lengths,
        held(query),
        held(new_key),
        held(new_value),
        held(key_cache),
        held(value_cache),
        held(residual),
        norm_gain.reshape(1, -1),
    )


def partial_products(k, rows, gate_rows, up_rows, after):
    count = rows.shape[0]
    units = gate_rows.shape[0]
    half = count // 2
    valid = min(WIDTH, units - k * WIDTH)
    step = 256
    steps = WIDTH // step
    depth = gate_rows.shape[1]
    columns = chunk_columns(k)

    def kernel(rows_ref, gate_ref, up_ref, *rest):
        out_ref, in_ref = rest[-2:]
        i = pl.program_id(0)
        if columns > TWO:
            out_ref[:, TWO:] = rest[0][:half]
            in_ref[:, TWO:] = rest[0][half:]
        for weight, offset in ((gate_ref, 0), (up_ref, WIDTH)):
            part = lax.dot_general(rows_ref[...], weight[...], (((1,), (1,)), ((), ())), preferred_element_type=f32)
            if valid < WIDTH:
                unit = lax.broadcasted_iota(jnp.int32, part.shape, 1) + i * step
                part = jnp.where(unit < valid, part, 0.0)
            part = part.astype(bf16)
            at = pl.ds(pl.multiple_of(offset + i * step, step), step)
            out_ref[:, at] = part[:half]
            in_ref[:, at] = part[half:]

    shape = jax.ShapeDtypeStruct((half, columns), bf16)
    first = k * steps
    return pl.pallas_call(
        kernel,
        grid=(steps,),
        in_specs=[
            pl.BlockSpec((count, depth), lambda i: (0, 0)),
            pl.BlockSpec((step, depth), lambda i: (first + i, 0)),
            pl.BlockSpec((step, depth), lambda i: (first + i, 0)),
        ]
        + ([pl.BlockSpec((count, LANES), lambda i: (0, depth // LANES))] if columns > TWO else [])
        + [ANY] * len(after),
        out_specs=[pl.BlockSpec((half, columns), lambda i: (0, 0))] * 2,
        out_shape=[shape, shape],
        compiler_params=pltpu.CompilerParams(vmem_limit_bytes=24 << 20),
        cost_estimate=cost(4 * count * depth * WIDTH, 4 * depth * WIDTH + 6 * count * WIDTH),
        name="partial_products",
    )(rows, gate_rows, up_rows, *([rows] if columns > TWO else []), *after)


def hop(outer, inv_in, s, t, count, got_e, got_m, part_out, part_in, after):
    half = part_out[0].shape[0]

    def inside(j):
        return 0 <= j < count

    def columns(*js):
        return max([chunk_columns(2 * j + s) for j in js if inside(j)], default=0)

    def hid_e(step):
        return inside(step - 3) or inside(step - 5)

    names, operands, specs = ["outer"], [outer], [SMEM]

    def add(name, value):
        names.append(name)
        operands.append(value)
        specs.append(VMEM)

    if columns(t, t - 2) or hid_e(t):
        add("got_e", got_e)
    if got_m is not None and (inside(t - 1) or inside(t - 4)):
        add("got_m", got_m)
    if inside(t + 1):
        add("next_out", part_out[t + 1])
    if inside(t):
        add("out", part_out[t])
    if inside(t - 1):
        add("in1", part_in[t - 1])
    starts_inv = inside(t - 2) and columns(t - 2) > TWO
    if inside(t - 2):
        add("in2", part_in[t - 2])
        if not starts_inv:
            add("inv", inv_in)
    operands += after
    specs += [ANY] * len(after)
    nxt = t + 1
    hid_at_e = columns(nxt, nxt - 2)
    hid_at_got_e = columns(t, t - 2)
    width_e = hid_at_e + (WIDTH if hid_e(nxt) else 0)
    hid_at_m = columns(t)
    hid_at_got_m = columns(t - 1)
    width_m = hid_at_m + (WIDTH if inside(t - 3) else 0)
    widths = [w for w in (width_e, width_m) if w]

    def kernel(*refs):
        r = dict(zip(names, refs))
        outs = list(refs[len(operands) :])
        to_e = outs.pop(0) if width_e else None
        to_m = outs.pop(0) if width_m else None

        def both(own, received, to, j):
            to[:, :TWO] = (own[:, :TWO].astype(f32) + received[:, :TWO].astype(f32)).astype(bf16)
            if columns(j) > TWO:
                to[:, TWO : columns(j)] = add_in_three(own[:, TWO:], received[:, TWO : columns(j)])[1]

        @pl.when(r["outer"][0] != 0)
        def _():
            if inside(t + 1):
                to_e[:, :TWO] = r["next_out"][:, :TWO]
            if inside(t - 2):
                if starts_inv:
                    squares, _ = add_in_three(r["in2"][:, TWO:], r["got_e"][:, TWO : TWO + LANES])
                    inv = lax.rsqrt(squares / D + eps)
                    outs[0][...] = inv
                else:
                    inv = r["inv"][...]
                gate = (r["in2"][:, :WIDTH].astype(f32) + r["got_e"][:, :WIDTH].astype(f32)) * inv
                up = (r["in2"][:, WIDTH:TWO].astype(f32) + r["got_e"][:, WIDTH:TWO].astype(f32)) * inv
                to_e[:, hid_at_e : hid_at_e + WIDTH] = (gate / (1.0 + jnp.exp(-gate)) * up).astype(bf16)

        @pl.when(r["outer"][0] == 0)
        def _():
            if inside(t - 1):
                both(r["in1"], r["got_m"], to_e, t - 1)
            if inside(t - 4):
                to_e[:, hid_at_e : hid_at_e + WIDTH] = r["got_m"][:, hid_at_got_m : hid_at_got_m + WIDTH]
            if inside(t):
                both(r["out"], r["got_e"], to_m, t)
            if inside(t - 3):
                to_m[:, hid_at_m : hid_at_m + WIDTH] = r["got_e"][:, hid_at_got_e : hid_at_got_e + WIDTH]
            if starts_inv:
                outs[0][...] = jnp.zeros(outs[0].shape, f32)

    shapes = [jax.ShapeDtypeStruct((half, w), bf16) for w in widths]
    if starts_inv:
        shapes.append(jax.ShapeDtypeStruct((half, 1), f32))
    outs = pl.pallas_call(
        kernel,
        in_specs=specs,
        out_specs=[VMEM] * len(shapes),
        out_shape=shapes,
        compiler_params=pltpu.CompilerParams(vmem_limit_bytes=24 << 20),
        cost_estimate=cost(8 * half * TWO, 10 * half * TWO),
        name="hop",
    )(*operands)
    outs = list(outs)
    to_e = (outs.pop(0), hid_at_e) if width_e else None
    to_m = (outs.pop(0), hid_at_m) if width_m else None
    return to_e, to_m, outs[0] if outs else inv_in


def hidden_rows(outer, buffers, after):
    half = buffers[0][0].shape[0]

    def kernel(outer_ref, sent, got, from_m, late, *rest):
        hid = rest[-1]

        @pl.when(outer_ref[0] != 0)
        def _():
            hid[:half] = late[:, buffers[3][1] : buffers[3][1] + WIDTH]
            hid[half:] = sent[:, buffers[0][1] : buffers[0][1] + WIDTH]

        @pl.when(outer_ref[0] == 0)
        def _():
            hid[:half] = from_m[:, buffers[2][1] : buffers[2][1] + WIDTH]
            hid[half:] = got[:, buffers[1][1] : buffers[1][1] + WIDTH]

    return pl.pallas_call(
        kernel,
        in_specs=[SMEM] + [VMEM] * 4 + [ANY] * len(after),
        out_specs=VMEM,
        out_shape=jax.ShapeDtypeStruct((2 * half, WIDTH), bf16),
        compiler_params=pltpu.CompilerParams(vmem_limit_bytes=24 << 20),
        name="hidden_rows",
    )(outer, *[buffer for buffer, _ in buffers], *after)


def down_product(total, k, hidden, w_down):
    first, last = k * WIDTH, min((k + 1) * WIDTH, w_down.shape[0])
    term = jnp.dot(hidden[:, : last - first], w_down[first:last], preferred_element_type=f32)
    return term if total is None else total + term


def mlp_line(scaled, w_gate, w_up, w_down):
    place = lax.axis_index("mix")
    left = place < 2
    outer = ((place == 0) | (place == 3)).astype(jnp.int32).reshape(1)

    across = swap(scaled, "ffn")
    beside = swap(scaled, "pair")
    diagonal = swap(across, "pair")
    here = jnp.concatenate([scaled, across])
    there = jnp.concatenate([beside, diagonal])
    rows = jnp.concatenate([jnp.where(left, here, there), jnp.where(left, there, here)])
    half = here.shape[0]

    gate_rows = pltpu.with_memory_space_constraint(w_gate.T, pltpu.HBM)
    up_rows = pltpu.with_memory_space_constraint(w_up.T, pltpu.HBM)
    chunks = -(-gate_rows.shape[0] // WIDTH)
    counts = (-(-chunks // 2), chunks // 2)
    part_out, part_in = ({}, {}), ({}, {})
    sent, got = {}, {}

    def products(k, after):
        if k < chunks:
            a, b = partial_products(k, rows, gate_rows, up_rows, after)
            part_out[k % 2][k // 2], part_in[k % 2][k // 2] = a, b
            return [a]
        return after

    def send(s, t, to_e, to_m):
        sent["e", s, t], sent["m", s, t] = to_e, to_m
        got["e", s, t] = (outward(to_e[0]), to_e[1]) if to_e else None
        got["m", s, t] = (middle(to_m[0]), to_m[1]) if to_m else None

    def hidden_of(k):
        s, j = k % 2, k // 2
        return [sent["e", s, j + 3], got["e", s, j + 3], got["m", s, j + 4], got["e", s, j + 5]]

    after = products(0, [])
    send(0, 0, (part_out[0][0], TWO), None)
    after = products(1, after)
    send(1, 0, (part_out[1][0], TWO), None)
    after = products(2, after)
    total, inv_in = None, None
    for t in range(counts[0] + 5):
        for s in (0, 1):
            count = counts[s]
            if t < count + 4:
                got_e, got_m = got["e", s, t], got["m", s, t]
                to_e, to_m, inv_in = hop(
                    outer,
                    inv_in,
                    s,
                    t,
                    count,
                    got_e and got_e[0],
                    got_m and got_m[0],
                    part_out[s],
                    part_in[s],
                    after,
                )
                send(s, t + 1, to_e, to_m)
                after = [(to_e or to_m)[0]]
            after = products(2 * t + s + 3, after)
            if 0 <= t - 5 < count:
                k = 2 * (t - 5) + s
                hidden = hidden_rows(outer, hidden_of(k), after + ([] if total is None else [total]))
                total = down_product(total, k, hidden, w_down)
                after = [hidden]
    total = total.astype(bf16)
    far, near = total[:half], total[half:]
    for_here = jnp.where(left, far, near)
    for_there = jnp.where(left, near, far)
    chip = for_here.astype(f32) + swap(for_there, "pair").astype(f32)
    block = half // 2
    return chip[:block] + swap(chip[block:].astype(bf16), "ffn").astype(f32)


def mlp_sums(normed, w_gate, w_up, w_down):
    gathered = lax.all_gather(normed, ("ffn", "pair"), axis=0, tiled=True)
    parts = []
    for weight in (w_gate, w_up):
        part = jnp.dot(gathered, weight, preferred_element_type=jnp.float32).astype(jnp.bfloat16)
        parts.append(lax.psum_scatter(part, "mix", scatter_dimension=0, tiled=True).astype(jnp.float32))
    hidden = (jax.nn.silu(parts[0]) * parts[1]).astype(jnp.bfloat16)
    hidden = lax.all_gather(hidden, "mix", axis=0, tiled=True)
    partial_value = jnp.dot(hidden, w_down, preferred_element_type=jnp.float32)
    return lax.psum_scatter(
        partial_value.astype(jnp.bfloat16), ("ffn", "pair"), scatter_dimension=0, tiled=True
    ).astype(jnp.float32)


def per_device(
    on_line,
    query,
    new_key,
    new_value,
    key_cache,
    value_cache,
    lengths,
    counts,
    residual,
    norm_gain,
    w_gate,
    w_up,
    w_down,
):
    if on_line:
        x, scaled = attend_rows(
            query, new_key, new_value, key_cache, value_cache, lengths, residual, norm_gain
        )
        mlp = mlp_line(scaled, w_gate, w_up, w_down)
    else:
        x = residual.astype(f32) + attend(query, new_key, new_value, key_cache, value_cache, lengths)
        inv = lax.rsqrt(lax.psum(jnp.sum(x * x, axis=1, keepdims=True), "mix") / D + eps)
        normed = (x * inv * norm_gain.astype(f32)).astype(bf16)
        mlp = mlp_sums(normed, w_gate, w_up, w_down)
    slots = jnp.arange(x.shape[0], dtype=jnp.int32)
    live = slots < counts[0]
    return jnp.where(live[:, None], x + mlp, jnp.zeros_like(x)).astype(jnp.bfloat16)


def solution(mesh):
    sizes = mesh.shape
    on_line = sizes["mix"] == 4 and sizes["ffn"] == 2 and sizes["pair"] == 2
    placed = (
        P(("grp", "ffn", "pair"), "mix"),
        P(("grp", "ffn", "pair"), "mix"),
        P(("grp", "ffn", "pair"), "mix"),
        P(("grp", "ffn", "pair"), None, "mix"),
        P(("grp", "ffn", "pair"), None, "mix"),
        P(("grp", "ffn", "pair")),
        P(("grp", "ffn", "pair")),
        P(("grp", "ffn", "pair"), "mix"),
        P("mix"),
        P("mix", ("ffn", "pair")),
        P("mix", ("ffn", "pair")),
        P(("ffn", "pair"), "mix"),
    )
    return jax.shard_map(
        functools.partial(per_device, on_line),
        mesh=mesh,
        in_specs=placed,
        out_specs=P(("grp", "ffn", "pair"), "mix"),
        check_vma=False,
    )
```

```python
import functools

import jax
import jax.numpy as jnp
from jax import lax
from jax.experimental import pallas as pl
from jax.experimental.pallas import tpu as pltpu
from jax.sharding import PartitionSpec as P

D = 8192
HD = 128


eps = 1e-05


def attend(query, new_key, new_value, key_cache, value_cache, lengths):
    rows = query.shape[0]
    heads = query.shape[1] // HD
    cache_len = key_cache.shape[1]
    scale = 1.0 / HD**0.5
    q_heads = query.reshape(rows, heads, HD)
    k_all = key_cache.reshape(rows, cache_len, heads, HD)
    v_all = value_cache.reshape(rows, cache_len, heads, HD)
    scores = jnp.einsum("chd,cphd->chp", q_heads, k_all, preferred_element_type=jnp.float32) * scale
    own = (
        jnp.einsum(
            "chd,chd->ch",
            q_heads,
            new_key.reshape(rows, heads, HD),
            preferred_element_type=jnp.float32,
        )
        * scale
    )
    valid = jnp.arange(cache_len, dtype=jnp.int32)[None, :] < lengths[:, None]
    scores = jnp.where(valid[:, None, :], scores, -jnp.inf)
    top = jnp.maximum(jnp.max(scores, axis=-1), own)
    weights = jnp.exp(scores - top[..., None])
    own_w = jnp.exp(own - top)
    total = jnp.sum(weights, axis=-1) + own_w
    probs = (weights / total[..., None]).astype(jnp.bfloat16)
    own_p = (own_w / total).astype(jnp.bfloat16)
    mixed = jnp.einsum("chp,cphd->chd", probs, v_all, preferred_element_type=jnp.float32)
    own_v = new_value.reshape(rows, heads, HD).astype(jnp.float32)
    mixed = mixed + own_p.astype(jnp.float32)[..., None] * own_v
    return mixed.reshape(rows, heads * HD)


LANES = 128
WIDTH = 384
PARTS = 1
SCALE = 2
OUTWARD = ((0, 1), (1, 0), (2, 3), (3, 2))
ACROSS = ((0, 2), (2, 0), (1, 3), (3, 1))
MIDDLE = ((0, 1), (1, 0), (2, 4), (4, 2), (3, 5), (5, 3), (6, 7), (7, 6))
SWAP = ((0, 1), (1, 0))
f32 = jnp.float32
bf16 = jnp.bfloat16
ANY = pl.BlockSpec(memory_space=pl.ANY)
SMEM = pl.BlockSpec(memory_space=pltpu.SMEM)
VMEM = pl.BlockSpec(memory_space=pltpu.VMEM)


def cost(flops, moved):
    return pl.CostEstimate(flops=int(flops * SCALE), bytes_accessed=int(moved * SCALE), transcendentals=0)


def outward(a):
    return lax.ppermute(a, "mix", OUTWARD)


def middle(a):
    return lax.ppermute(a, ("mix", "pair"), MIDDLE)


def swap(a, axis):
    return lax.ppermute(a, axis, SWAP)


class Chunk:
    def __init__(self, index, first, units):
        self.index, self.first, self.units = index, first, units
        self.width = -(-units // LANES) * LANES
        self.pair = 2 * self.width
        self.columns = self.pair + (LANES if index == 0 else 0)


def chunks_of(units):
    count = max(units // WIDTH, 1)
    starts = [k * WIDTH for k in range(count)] + [units]
    return [Chunk(k, starts[k], starts[k + 1] - starts[k]) for k in range(count)]


def in_three(total, shape):
    lane = lax.broadcasted_iota(jnp.int32, shape, 1)
    high = total.astype(bf16).astype(f32)
    middle_part = (total - high).astype(bf16).astype(f32)
    low = total - high - middle_part
    three = jnp.where(lane == 0, high, jnp.where(lane == 1, middle_part, jnp.where(lane == 2, low, 0.0)))
    return three.astype(bf16)


def add_in_three(a, b):
    lane = lax.broadcasted_iota(jnp.int32, a.shape, 1)
    total = jnp.sum(jnp.where(lane < 3, a.astype(f32) + b.astype(f32), 0.0), axis=1, keepdims=True)
    return total, in_three(total, a.shape)


def attend_rows(part, parts, query, new_key, new_value, key_cache, value_cache, lengths, residual, norm_gain, after):
    features = query.shape[1]
    rows = query.shape[0] // parts
    heads = features // HD
    cache_len = key_cache.shape[1]
    block = 16
    tall, wide = heads * block, block * cache_len
    begin = part * (rows // block)
    scale = 1.0 / HD**0.5
    held = functools.partial(pltpu.with_memory_space_constraint, memory_space=pltpu.HBM)

    def kernel(length_ref, q_ref, nk_ref, nv_ref, k_ref, v_ref, res_ref, gain_ref, *rest):
        x_ref, scaled_ref, sparse = rest[-3:]

        @pl.when(pl.program_id(0) == 0)
        def _():
            sparse[...] = jnp.zeros_like(sparse)

        for h in range(heads):
            sparse[h * block : (h + 1) * block, h * HD : (h + 1) * HD] = q_ref[:, h * HD : (h + 1) * HD]
        q_rows = sparse[...]
        over = (((1,), (1,)), ((), ()))
        keys = k_ref[...].reshape(wide, features)
        scores = lax.dot_general(q_rows, keys, over, preferred_element_type=f32) * scale
        own = lax.dot_general(q_rows, nk_ref[...], over, preferred_element_type=f32) * scale
        mine = lax.broadcasted_iota(jnp.int32, own.shape, 0) % block == lax.broadcasted_iota(jnp.int32, own.shape, 1)
        own = jnp.sum(jnp.where(mine, own, 0.0), axis=1, keepdims=True)
        column = lax.broadcasted_iota(jnp.int32, scores.shape, 1)
        owner = lax.broadcasted_iota(jnp.int32, scores.shape, 0) % block
        offset = column - owner * cache_len
        candidate = lax.broadcasted_iota(jnp.int32, (tall, 1), 0) % block
        span = jnp.zeros((tall, 1), jnp.int32)
        for c in range(block):
            span = jnp.where(candidate == c, length_ref[(pl.program_id(0) + begin) * block + c], span)
        valid = (offset >= 0) & (offset < span)
        scores = jnp.where(valid, scores, -jnp.inf)
        top = jnp.maximum(jnp.max(scores, axis=1, keepdims=True), own)
        weights = jnp.exp(scores - top)
        own_w = jnp.exp(own - top)
        total = jnp.sum(weights, axis=1, keepdims=True) + own_w
        probs = (weights / total).astype(bf16)
        own_p = (own_w / total).astype(bf16).astype(f32)
        mixed = jnp.dot(probs, v_ref[...].reshape(wide, features), preferred_element_type=f32)
        squares = jnp.zeros((block, HD), f32)
        for h in range(heads):
            at, rows_at = slice(h * HD, (h + 1) * HD), slice(h * block, (h + 1) * block)
            x = res_ref[:, at].astype(f32) + mixed[rows_at, at] + own_p[rows_at] * nv_ref[:, at].astype(f32)
            x_ref[:, at] = x
            scaled_ref[:, at] = (x * gain_ref[:, at].astype(f32)).astype(bf16)
            squares = squares + x * x
        scaled_ref[:, features:] = in_three(jnp.sum(squares, axis=1, keepdims=True), (block, LANES))

    flat = pl.BlockSpec((block, features), lambda i: (begin + i, 0))
    cache = pl.BlockSpec((block, cache_len, features), lambda i: (begin + i, 0, 0))
    return pl.pallas_call(
        kernel,
        grid=(rows // block,),
        in_specs=[
            SMEM,
            flat,
            flat,
            flat,
            cache,
            cache,
            flat,
            pl.BlockSpec((1, features), lambda i: (0, 0)),
        ]
        + [ANY] * len(after),
        out_specs=[pl.BlockSpec((block, features), lambda i: (i, 0)), pl.BlockSpec((block, features + LANES), lambda i: (i, 0))],
        out_shape=[
            jax.ShapeDtypeStruct((rows, features), f32),
            jax.ShapeDtypeStruct((rows, features + LANES), bf16),
        ],
        scratch_shapes=[pltpu.VMEM((tall, features), bf16)],
        compiler_params=pltpu.CompilerParams(vmem_limit_bytes=40 << 20),
        cost_estimate=pl.CostEstimate(
            flops=4 * rows // block * tall * wide * features,
            bytes_accessed=4 * rows * cache_len * features,
            transcendentals=rows // block * tall * wide,
        ),
        name="attend_rows",
    )(
        lengths,
        held(query),
        held(new_key),
        held(new_value),
        held(key_cache),
        held(value_cache),
        held(residual),
        norm_gain.reshape(1, -1),
        *after,
    )


def partial_products(chunk, rows, gate_rows, up_rows, after):
    count = rows.shape[0]
    depth = gate_rows.shape[1]
    half = count // 2
    width, pair, columns = chunk.width, chunk.pair, chunk.columns
    if chunk.first % WIDTH == 0 and width > WIDTH:
        tiles = [(chunk.first + at, min(WIDTH, width - at)) for at in range(0, width, WIDTH)]
    else:
        tiles = [(chunk.first, width)]
    if any(first % size for first, size in tiles):
        tiles = [(chunk.first + at, LANES) for at in range(0, width, LANES)]

    def kernel(rows_ref, *rest):
        out_ref, in_ref = rest[-2:]
        if columns > pair:
            squares = rest[2 * len(tiles)]
            out_ref[:, pair:] = squares[:half]
            in_ref[:, pair:] = squares[half:]
        for n, (first, size) in enumerate(tiles):
            for weight, offset in ((rest[2 * n], 0), (rest[2 * n + 1], width)):
                part = lax.dot_general(rows_ref[...], weight[...], (((1,), (1,)), ((), ())), preferred_element_type=f32)
                begin = first - chunk.first
                if begin + size > chunk.units:
                    unit = lax.broadcasted_iota(jnp.int32, part.shape, 1) + begin
                    part = jnp.where(unit < chunk.units, part, 0.0)
                part = part.astype(bf16)
                at = slice(offset + begin, offset + begin + size)
                out_ref[:, at] = part[:half]
                in_ref[:, at] = part[half:]

    brief = 0.5 if chunk.index < 2 else 1
    shape = jax.ShapeDtypeStruct((half, columns), bf16)
    weights, specs = [], []
    for first, size in tiles:
        weights += [gate_rows, up_rows]
        specs += [pl.BlockSpec((size, depth), functools.partial(lambda at, i: (at, 0), first // size))] * 2
    return pl.pallas_call(
        kernel,
        grid=(1,),
        in_specs=[pl.BlockSpec((count, depth), lambda i: (0, 0))]
        + specs
        + ([pl.BlockSpec((count, LANES), lambda i: (0, depth // LANES))] if columns > pair else [])
        + [ANY] * len(after),
        out_specs=[pl.BlockSpec((half, columns), lambda i: (0, 0))] * 2,
        out_shape=[shape, shape],
        compiler_params=pltpu.CompilerParams(vmem_limit_bytes=24 << 20),
        cost_estimate=cost(brief * 4 * count * depth * width, brief * (4 * depth * width + 6 * count * width)),
        name="partial_products",
    )(rows, *weights, *([rows] if columns > pair else []), *after)


def twin_products(chunks, rows, gate_rows, up_rows, after):
    count = rows.shape[0]
    depth = gate_rows.shape[1]
    half = count // 2
    width = chunks[0].width

    def kernel(rows_ref, gate_ref, up_ref, *rest):
        outs = rest[-2 * len(chunks) :]
        parts = []
        for weight in (gate_ref, up_ref):
            part = lax.dot_general(rows_ref[...], weight[...], (((1,), (1,)), ((), ())), preferred_element_type=f32)
            parts.append(part.astype(bf16))
        for c in range(len(chunks)):

            @pl.when(pl.program_id(0) == c)
            def _():
                for offset, part in zip((0, width), parts):
                    outs[2 * c][:, offset : offset + width] = part[:half]
                    outs[2 * c + 1][:, offset : offset + width] = part[half:]

    brief = 0.5 if chunks[0].index < 4 else 1
    first = chunks[0].first // width
    return pl.pallas_call(
        kernel,
        grid=(len(chunks),),
        in_specs=[
            pl.BlockSpec((count, depth), lambda i: (0, 0)),
            pl.BlockSpec((width, depth), lambda i: (first + i, 0)),
            pl.BlockSpec((width, depth), lambda i: (first + i, 0)),
        ]
        + [ANY] * len(after),
        out_specs=[pl.BlockSpec((half, 2 * width), lambda i: (0, 0))] * (2 * len(chunks)),
        out_shape=[jax.ShapeDtypeStruct((half, 2 * width), bf16)] * (2 * len(chunks)),
        compiler_params=pltpu.CompilerParams(vmem_limit_bytes=24 << 20),
        cost_estimate=cost(brief * 8 * count * depth * width, brief * (8 * depth * width + 12 * count * width)),
        name="twin_products",
    )(rows, gate_rows, up_rows, *after)


def hop(outer, inv_in, stream, t, got_e, got_m, part_out, part_in, after):
    half = part_out[0].shape[0]
    count = len(stream)

    def inside(j):
        return 0 <= j < count

    def columns(*js):
        return max([stream[j].columns for j in js if inside(j)], default=0)

    def wide(*js):
        return max([stream[j].width for j in js if inside(j)], default=0)

    def hid_e(step):
        return inside(step - 3) or inside(step - 5)

    names, operands, specs = ["outer"], [outer], [SMEM]

    def add(name, value):
        names.append(name)
        operands.append(value)
        specs.append(VMEM)

    if columns(t, t - 2) or hid_e(t):
        add("got_e", got_e)
    if got_m is not None and (inside(t - 1) or inside(t - 4)):
        add("got_m", got_m)
    if inside(t + 1):
        add("next_out", part_out[t + 1])
    if inside(t):
        add("out", part_out[t])
    if inside(t - 1):
        add("in1", part_in[t - 1])
    starts_inv = inside(t - 2) and stream[t - 2].columns > stream[t - 2].pair
    if inside(t - 2):
        add("in2", part_in[t - 2])
        if not starts_inv:
            add("inv", inv_in)
    operands += after
    specs += [ANY] * len(after)
    nxt = t + 1
    hid_at_e = columns(nxt, nxt - 2)
    hid_at_got_e = columns(t, t - 2)
    width_e = hid_at_e + wide(nxt - 3, nxt - 5)
    hid_at_m = columns(t)
    hid_at_got_m = columns(t - 1)
    width_m = hid_at_m + wide(t - 3)
    widths = [w for w in (width_e, width_m) if w]

    def kernel(*refs):
        r = dict(zip(names, refs))
        outs = list(refs[len(operands) :])
        to_e = outs.pop(0) if width_e else None
        to_m = outs.pop(0) if width_m else None

        def both(own, received, to, j):
            pair, end = stream[j].pair, stream[j].columns
            to[:, :pair] = (own[:, :pair].astype(f32) + received[:, :pair].astype(f32)).astype(bf16)
            if end > pair:
                to[:, pair:end] = add_in_three(own[:, pair:], received[:, pair:end])[1]

        @pl.when(r["outer"][0] != 0)
        def _():
            if inside(t + 1):
                pair = stream[t + 1].pair
                to_e[:, :pair] = r["next_out"][:, :pair]
            if inside(t - 2):
                w, pair = stream[t - 2].width, stream[t - 2].pair
                if starts_inv:
                    squares, _ = add_in_three(r["in2"][:, pair:], r["got_e"][:, pair : pair + LANES])
                    inv = lax.rsqrt(squares / D + eps)
                    outs[0][...] = inv
                else:
                    inv = r["inv"][...]
                gate = (r["in2"][:, :w].astype(f32) + r["got_e"][:, :w].astype(f32)) * inv
                up = (r["in2"][:, w:pair].astype(f32) + r["got_e"][:, w:pair].astype(f32)) * inv
                to_e[:, hid_at_e : hid_at_e + w] = (gate / (1.0 + jnp.exp(-gate)) * up).astype(bf16)

        @pl.when(r["outer"][0] == 0)
        def _():
            if inside(t - 1):
                both(r["in1"], r["got_m"], to_e, t - 1)
            if inside(t - 4):
                w = stream[t - 4].width
                to_e[:, hid_at_e : hid_at_e + w] = r["got_m"][:, hid_at_got_m : hid_at_got_m + w]
            if inside(t):
                both(r["out"], r["got_e"], to_m, t)
            if inside(t - 3):
                w = stream[t - 3].width
                to_m[:, hid_at_m : hid_at_m + w] = r["got_e"][:, hid_at_got_e : hid_at_got_e + w]
            if starts_inv:
                outs[0][...] = jnp.zeros(outs[0].shape, f32)

    shapes = [jax.ShapeDtypeStruct((half, w), bf16) for w in widths]
    if starts_inv:
        shapes.append(jax.ShapeDtypeStruct((half, 1), f32))
    outs = pl.pallas_call(
        kernel,
        in_specs=specs,
        out_specs=[VMEM] * len(shapes),
        out_shape=shapes,
        compiler_params=pltpu.CompilerParams(vmem_limit_bytes=24 << 20),
        cost_estimate=cost(16 * half * WIDTH, 20 * half * WIDTH),
        name="hop",
    )(*operands)
    outs = list(outs)
    to_e = (outs.pop(0), hid_at_e) if width_e else None
    to_m = (outs.pop(0), hid_at_m) if width_m else None
    return to_e, to_m, outs[0] if outs else inv_in


def hidden_rows(outer, width, buffers, after):
    half = buffers[0][0].shape[0]

    def kernel(outer_ref, sent, got, from_m, late, *rest):
        hid = rest[-1]

        @pl.when(outer_ref[0] != 0)
        def _():
            hid[:half] = late[:, buffers[3][1] : buffers[3][1] + width]
            hid[half:] = sent[:, buffers[0][1] : buffers[0][1] + width]

        @pl.when(outer_ref[0] == 0)
        def _():
            hid[:half] = from_m[:, buffers[2][1] : buffers[2][1] + width]
            hid[half:] = got[:, buffers[1][1] : buffers[1][1] + width]

    return pl.pallas_call(
        kernel,
        in_specs=[SMEM] + [VMEM] * 4 + [ANY] * len(after),
        out_specs=VMEM,
        out_shape=jax.ShapeDtypeStruct((2 * half, width), bf16),
        compiler_params=pltpu.CompilerParams(vmem_limit_bytes=24 << 20),
        name="hidden_rows",
    )(outer, *[buffer for buffer, _ in buffers], *after)


def down_product(total, chunk, hidden, w_down):
    weight = w_down[chunk.first : chunk.first + chunk.units]
    term = jnp.dot(hidden[:, : chunk.units], weight, preferred_element_type=f32)
    return term if total is None else total + term


def mlp_line(scaled, w_gate, w_up, w_down):
    place = lax.axis_index("mix")
    left = place < 2
    outer = ((place == 0) | (place == 3)).astype(jnp.int32).reshape(1)

    across = [swap(part, "ffn") for part in scaled]
    beside = [swap(part, "pair") for part in scaled]
    diagonal = [swap(part, "pair") for part in across]
    here = jnp.concatenate(scaled + across)
    there = jnp.concatenate(beside + diagonal)
    rows = jnp.concatenate([jnp.where(left, here, there), jnp.where(left, there, here)])
    half = here.shape[0]

    gate_rows = pltpu.with_memory_space_constraint(w_gate.T, pltpu.HBM)
    up_rows = pltpu.with_memory_space_constraint(w_up.T, pltpu.HBM)
    chunks = chunks_of(gate_rows.shape[0])
    streams = (chunks[0::2], chunks[1::2])
    part_out, part_in = ({}, {}), ({}, {})
    sent, got = {}, {}

    def products(k, after):
        if k >= len(chunks) or k // 2 in part_out[k % 2]:
            return after
        if k >= 2 and k % 2 == 0 and k + 1 < len(chunks) and chunks[k + 1].units == chunks[k].width:
            made = twin_products(chunks[k : k + 2], rows, gate_rows, up_rows, after)
            part_out[1][k // 2], part_in[1][k // 2] = made[2:]
        else:
            made = partial_products(chunks[k], rows, gate_rows, up_rows, after)
        part_out[k % 2][k // 2], part_in[k % 2][k // 2] = made[:2]
        return [made[0]]

    def send(s, t, to_e, to_m):
        sent["e", s, t], sent["m", s, t] = to_e, to_m
        got["e", s, t] = (outward(to_e[0]), to_e[1]) if to_e else None
        got["m", s, t] = (middle(to_m[0]), to_m[1]) if to_m else None

    def hidden_of(k):
        s, j = k % 2, k // 2
        return [sent["e", s, j + 3], got["e", s, j + 3], got["m", s, j + 4], got["e", s, j + 5]]

    after = products(0, [])
    send(0, 0, (part_out[0][0], 0), None)
    after = products(1, after)
    send(1, 0, (part_out[1][0], 0), None)
    after = products(2, after)
    total, inv_in = None, None
    for t in range(len(streams[0]) + 5):
        for s in (0, 1):
            count = len(streams[s])
            if t < count + 4:
                got_e, got_m = got["e", s, t], got["m", s, t]
                to_e, to_m, inv_in = hop(
                    outer,
                    inv_in,
                    streams[s],
                    t,
                    got_e and got_e[0],
                    got_m and got_m[0],
                    part_out[s],
                    part_in[s],
                    after,
                )
                send(s, t + 1, to_e, to_m)
                after = [(to_e or to_m)[0]]
            k = 2 * t + s + 3
            if k < len(chunks) and k // 2 in part_out[k % 2]:
                k += 1
            after = products(k, after)
            if 0 <= t - 5 < count:
                k = 2 * (t - 5) + s
                hidden = hidden_rows(outer, chunks[k].width, hidden_of(k), after + ([] if total is None else [total]))
                total = down_product(total, chunks[k], hidden, w_down)
                after = [hidden]
    total = total.astype(bf16)
    far, near = total[:half], total[half:]
    for_here = jnp.where(left, far, near)
    for_there = jnp.where(left, near, far)
    chip = for_here.astype(f32) + swap(for_there, "pair").astype(f32)
    block = half // 2
    return chip[:block] + swap(chip[block:].astype(bf16), "ffn").astype(f32)


def mlp_sums(normed, w_gate, w_up, w_down):
    gathered = lax.all_gather(normed, ("ffn", "pair"), axis=0, tiled=True)
    parts = []
    for weight in (w_gate, w_up):
        part = jnp.dot(gathered, weight, preferred_element_type=jnp.float32).astype(jnp.bfloat16)
        parts.append(lax.psum_scatter(part, "mix", scatter_dimension=0, tiled=True).astype(jnp.float32))
    hidden = (jax.nn.silu(parts[0]) * parts[1]).astype(jnp.bfloat16)
    hidden = lax.all_gather(hidden, "mix", axis=0, tiled=True)
    partial_value = jnp.dot(hidden, w_down, preferred_element_type=jnp.float32)
    return lax.psum_scatter(
        partial_value.astype(jnp.bfloat16), ("ffn", "pair"), scatter_dimension=0, tiled=True
    ).astype(jnp.float32)


def per_device(
    on_line,
    query,
    new_key,
    new_value,
    key_cache,
    value_cache,
    lengths,
    counts,
    residual,
    norm_gain,
    w_gate,
    w_up,
    w_down,
):
    if on_line:
        xs, scaled, after = [], [], []
        for part in range(PARTS):
            x, ready = attend_rows(
                part,
                PARTS,
                query,
                new_key,
                new_value,
                key_cache,
                value_cache,
                lengths,
                residual,
                norm_gain,
                after,
            )
            xs.append(x)
            scaled.append(ready)
            after = [ready]
        x = jnp.concatenate(xs)
        mlp = mlp_line(scaled, w_gate, w_up, w_down)
    else:
        x = residual.astype(f32) + attend(query, new_key, new_value, key_cache, value_cache, lengths)
        inv = lax.rsqrt(lax.psum(jnp.sum(x * x, axis=1, keepdims=True), "mix") / D + eps)
        normed = (x * inv * norm_gain.astype(f32)).astype(bf16)
        mlp = mlp_sums(normed, w_gate, w_up, w_down)
    slots = jnp.arange(x.shape[0], dtype=jnp.int32)
    live = slots < counts[0]
    return jnp.where(live[:, None], x + mlp, jnp.zeros_like(x)).astype(jnp.bfloat16)


def solution(mesh):
    sizes = mesh.shape
    on_line = sizes["mix"] == 4 and sizes["ffn"] == 2 and sizes["pair"] == 2
    placed = (
        P(("grp", "ffn", "pair"), "mix"),
        P(("grp", "ffn", "pair"), "mix"),
        P(("grp", "ffn", "pair"), "mix"),
        P(("grp", "ffn", "pair"), None, "mix"),
        P(("grp", "ffn", "pair"), None, "mix"),
        P(("grp", "ffn", "pair")),
        P(("grp", "ffn", "pair")),
        P(("grp", "ffn", "pair"), "mix"),
        P("mix"),
        P("mix", ("ffn", "pair")),
        P("mix", ("ffn", "pair")),
        P(("ffn", "pair"), "mix"),
    )
    return jax.shard_map(
        functools.partial(per_device, on_line),
        mesh=mesh,
        in_specs=placed,
        out_specs=P(("grp", "ffn", "pair"), "mix"),
        check_vma=False,
    )
```

```python
import functools

import jax
import jax.numpy as jnp
from jax import lax
from jax.experimental import pallas as pl
from jax.experimental.pallas import tpu as pltpu
from jax.sharding import PartitionSpec as P

D = 8192
HD = 128


eps = 1e-05


def attend(query, new_key, new_value, key_cache, value_cache, lengths):
    rows = query.shape[0]
    heads = query.shape[1] // HD
    cache_len = key_cache.shape[1]
    scale = 1.0 / HD**0.5
    q_heads = query.reshape(rows, heads, HD)
    k_all = key_cache.reshape(rows, cache_len, heads, HD)
    v_all = value_cache.reshape(rows, cache_len, heads, HD)
    scores = jnp.einsum("chd,cphd->chp", q_heads, k_all, preferred_element_type=jnp.float32) * scale
    own = (
        jnp.einsum(
            "chd,chd->ch",
            q_heads,
            new_key.reshape(rows, heads, HD),
            preferred_element_type=jnp.float32,
        )
        * scale
    )
    valid = jnp.arange(cache_len, dtype=jnp.int32)[None, :] < lengths[:, None]
    scores = jnp.where(valid[:, None, :], scores, -jnp.inf)
    top = jnp.maximum(jnp.max(scores, axis=-1), own)
    weights = jnp.exp(scores - top[..., None])
    own_w = jnp.exp(own - top)
    total = jnp.sum(weights, axis=-1) + own_w
    probs = (weights / total[..., None]).astype(jnp.bfloat16)
    own_p = (own_w / total).astype(jnp.bfloat16)
    mixed = jnp.einsum("chp,cphd->chd", probs, v_all, preferred_element_type=jnp.float32)
    own_v = new_value.reshape(rows, heads, HD).astype(jnp.float32)
    mixed = mixed + own_p.astype(jnp.float32)[..., None] * own_v
    return mixed.reshape(rows, heads * HD)


LANES = 128
WIDTH = 384
PARTS = 1
SCALE = 2
OUTWARD = ((0, 1), (1, 0), (2, 3), (3, 2))
ACROSS = ((0, 2), (2, 0), (1, 3), (3, 1))
MIDDLE = ((0, 1), (1, 0), (2, 4), (4, 2), (3, 5), (5, 3), (6, 7), (7, 6))
SWAP = ((0, 1), (1, 0))
f32 = jnp.float32
bf16 = jnp.bfloat16
ANY = pl.BlockSpec(memory_space=pl.ANY)
SMEM = pl.BlockSpec(memory_space=pltpu.SMEM)
VMEM = pl.BlockSpec(memory_space=pltpu.VMEM)


def cost(flops, moved):
    return pl.CostEstimate(flops=int(flops * SCALE), bytes_accessed=int(moved * SCALE), transcendentals=0)


def outward(a):
    return lax.ppermute(a, "mix", OUTWARD)


def middle(a):
    return lax.ppermute(a, ("mix", "pair"), MIDDLE)


def swap(a, axis):
    return lax.ppermute(a, axis, SWAP)


class Chunk:
    def __init__(self, index, first, units):
        self.index, self.first, self.units = index, first, units
        self.width = -(-units // LANES) * LANES
        self.pair = 2 * self.width
        self.columns = self.pair + (LANES if index == 0 else 0)


def chunks_of(units):
    count = max(units // WIDTH, 1)
    starts = [k * WIDTH for k in range(count)] + [units]
    return [Chunk(k, starts[k], starts[k + 1] - starts[k]) for k in range(count)]


def in_three(total, shape):
    lane = lax.broadcasted_iota(jnp.int32, shape, 1)
    high = total.astype(bf16).astype(f32)
    middle_part = (total - high).astype(bf16).astype(f32)
    low = total - high - middle_part
    three = jnp.where(lane == 0, high, jnp.where(lane == 1, middle_part, jnp.where(lane == 2, low, 0.0)))
    return three.astype(bf16)


def add_in_three(a, b):
    lane = lax.broadcasted_iota(jnp.int32, a.shape, 1)
    total = jnp.sum(jnp.where(lane < 3, a.astype(f32) + b.astype(f32), 0.0), axis=1, keepdims=True)
    return total, in_three(total, a.shape)


def attend_rows(part, parts, query, new_key, new_value, key_cache, value_cache, lengths, residual, norm_gain, after):
    features = query.shape[1]
    rows = query.shape[0] // parts
    heads = features // HD
    cache_len = key_cache.shape[1]
    block = 16
    few = block // 2
    tall, wide = heads * few, few * cache_len
    begin = part * (rows // block)
    scale = 1.0 / HD**0.5
    held = functools.partial(pltpu.with_memory_space_constraint, memory_space=pltpu.HBM)

    def kernel(length_ref, q_ref, nk_ref, nv_ref, k_ref, v_ref, res_ref, gain_ref, *rest):
        x_ref, scaled_ref, sparse = rest[-3:]

        @pl.when(pl.program_id(0) == 0)
        def _():
            sparse[...] = jnp.zeros_like(sparse)

        over = (((1,), (1,)), ((), ()))
        shares = []
        for sub in range(2):
            mine_at = slice(sub * few, (sub + 1) * few)
            for h in range(0, heads, 2):
                for odd in range(2):
                    at = slice((h + odd) * HD, (h + odd + 1) * HD)
                    part = q_ref[:, at].astype(f32)[mine_at]
                    none = jnp.zeros_like(part)
                    both = jnp.concatenate([none, part] if odd else [part, none])
                    sparse[sub, h * few : (h + 2) * few, at] = both.astype(bf16)
            q_rows = sparse[sub]
            keys = k_ref[mine_at].reshape(wide, features)
            scores = lax.dot_general(q_rows, keys, over, preferred_element_type=f32) * scale
            own = lax.dot_general(q_rows, nk_ref[...], over, preferred_element_type=f32) * scale
            row = lax.broadcasted_iota(jnp.int32, own.shape, 0) % few
            mine = row + sub * few == lax.broadcasted_iota(jnp.int32, own.shape, 1)
            own = jnp.sum(jnp.where(mine, own, 0.0), axis=1, keepdims=True)
            column = lax.broadcasted_iota(jnp.int32, scores.shape, 1)
            owner = lax.broadcasted_iota(jnp.int32, scores.shape, 0) % few
            offset = column - owner * cache_len
            candidate = lax.broadcasted_iota(jnp.int32, (tall, 1), 0) % few
            span = jnp.zeros((tall, 1), jnp.int32)
            for c in range(few):
                length = length_ref[(pl.program_id(0) + begin) * block + sub * few + c]
                span = jnp.where(candidate == c, length, span)
            valid = (offset >= 0) & (offset < span)
            scores = jnp.where(valid, scores, -jnp.inf)
            top = jnp.maximum(jnp.max(scores, axis=1, keepdims=True), own)
            weights = jnp.exp(scores - top)
            own_w = jnp.exp(own - top)
            total = jnp.sum(weights, axis=1, keepdims=True) + own_w
            probs = (weights / total).astype(bf16)
            own_p = (own_w / total).astype(bf16).astype(f32)
            mixed = jnp.dot(probs, v_ref[mine_at].reshape(wide, features), preferred_element_type=f32)
            shares.append((mixed, own_p))
        squares = jnp.zeros((block, HD), f32)
        for h in range(heads):
            at, rows_at = slice(h * HD, (h + 1) * HD), slice(h * few, (h + 1) * few)
            mixed = jnp.concatenate([share[0][rows_at, at] for share in shares])
            own_p = jnp.concatenate([share[1][rows_at] for share in shares])
            x = res_ref[:, at].astype(f32) + mixed + own_p * nv_ref[:, at].astype(f32)
            x_ref[:, at] = x
            scaled_ref[:, at] = (x * gain_ref[at].astype(f32)[None, :]).astype(bf16)
            squares = squares + x * x
        scaled_ref[:, features:] = in_three(jnp.sum(squares, axis=1, keepdims=True), (block, LANES))

    flat = pl.BlockSpec((block, features), lambda i: (begin + i, 0))
    cache = pl.BlockSpec((block, cache_len, features), lambda i: (begin + i, 0, 0))
    return pl.pallas_call(
        kernel,
        grid=(rows // block,),
        in_specs=[
            SMEM,
            flat,
            flat,
            flat,
            cache,
            cache,
            flat,
            pl.BlockSpec((features,), lambda i: (0,)),
        ]
        + [ANY] * len(after),
        out_specs=[pl.BlockSpec((block, features), lambda i: (i, 0)), pl.BlockSpec((block, features + LANES), lambda i: (i, 0))],
        out_shape=[
            jax.ShapeDtypeStruct((rows, features), f32),
            jax.ShapeDtypeStruct((rows, features + LANES), bf16),
        ],
        scratch_shapes=[pltpu.VMEM((2, tall, features), bf16)],
        compiler_params=pltpu.CompilerParams(vmem_limit_bytes=40 << 20),
        cost_estimate=pl.CostEstimate(
            flops=8 * rows // block * tall * wide * features,
            bytes_accessed=4 * rows * cache_len * features,
            transcendentals=2 * rows // block * tall * wide,
        ),
        name="attend_rows",
    )(
        lengths,
        held(query),
        held(new_key),
        held(new_value),
        held(key_cache),
        held(value_cache),
        held(residual),
        norm_gain,
        *after,
    )


def partial_products(chunk, rows, gate_rows, up_rows, after):
    count = rows.shape[0]
    depth = gate_rows.shape[1]
    half = count // 2
    width, pair, columns = chunk.width, chunk.pair, chunk.columns
    if chunk.first % WIDTH == 0 and width > WIDTH:
        tiles = [(chunk.first + at, min(WIDTH, width - at)) for at in range(0, width, WIDTH)]
    else:
        tiles = [(chunk.first, width)]
    if any(first % size for first, size in tiles):
        tiles = [(chunk.first + at, LANES) for at in range(0, width, LANES)]

    def kernel(rows_ref, *rest):
        out_ref, in_ref = rest[-2:]
        if columns > pair:
            squares = rest[2 * len(tiles)]
            out_ref[:, pair:] = squares[:half]
            in_ref[:, pair:] = squares[half:]
        for n, (first, size) in enumerate(tiles):
            for weight, offset in ((rest[2 * n], 0), (rest[2 * n + 1], width)):
                part = lax.dot_general(rows_ref[...], weight[...], (((1,), (1,)), ((), ())), preferred_element_type=f32)
                begin = first - chunk.first
                if begin + size > chunk.units:
                    unit = lax.broadcasted_iota(jnp.int32, part.shape, 1) + begin
                    part = jnp.where(unit < chunk.units, part, 0.0)
                part = part.astype(bf16)
                at = slice(offset + begin, offset + begin + size)
                out_ref[:, at] = part[:half]
                in_ref[:, at] = part[half:]

    brief = 0.5 if chunk.index < 2 else 1
    shape = jax.ShapeDtypeStruct((half, columns), bf16)
    weights, specs = [], []
    for first, size in tiles:
        weights += [gate_rows, up_rows]
        specs += [pl.BlockSpec((size, depth), functools.partial(lambda at, i: (at, 0), first // size))] * 2
    return pl.pallas_call(
        kernel,
        grid=(1,),
        in_specs=[pl.BlockSpec((count, depth), lambda i: (0, 0))]
        + specs
        + ([pl.BlockSpec((count, LANES), lambda i: (0, depth // LANES))] if columns > pair else [])
        + [ANY] * len(after),
        out_specs=[pl.BlockSpec((half, columns), lambda i: (0, 0))] * 2,
        out_shape=[shape, shape],
        compiler_params=pltpu.CompilerParams(vmem_limit_bytes=24 << 20),
        cost_estimate=cost(brief * 4 * count * depth * width, brief * (4 * depth * width + 6 * count * width)),
        name="partial_products",
    )(rows, *weights, *([rows] if columns > pair else []), *after)


def twin_products(chunks, rows, gate_rows, up_rows, after):
    count = rows.shape[0]
    depth = gate_rows.shape[1]
    half = count // 2
    width = chunks[0].width

    def kernel(rows_ref, gate_ref, up_ref, *rest):
        outs = rest[-2 * len(chunks) :]
        parts = []
        for weight in (gate_ref, up_ref):
            part = lax.dot_general(rows_ref[...], weight[...], (((1,), (1,)), ((), ())), preferred_element_type=f32)
            parts.append(part.astype(bf16))
        for c in range(len(chunks)):

            @pl.when(pl.program_id(0) == c)
            def _():
                for offset, part in zip((0, width), parts):
                    outs[2 * c][:, offset : offset + width] = part[:half]
                    outs[2 * c + 1][:, offset : offset + width] = part[half:]

    brief = 0.5 if chunks[0].index < 4 else 1
    first = chunks[0].first // width
    return pl.pallas_call(
        kernel,
        grid=(len(chunks),),
        in_specs=[
            pl.BlockSpec((count, depth), lambda i: (0, 0)),
            pl.BlockSpec((width, depth), lambda i: (first + i, 0)),
            pl.BlockSpec((width, depth), lambda i: (first + i, 0)),
        ]
        + [ANY] * len(after),
        out_specs=[pl.BlockSpec((half, 2 * width), lambda i: (0, 0))] * (2 * len(chunks)),
        out_shape=[jax.ShapeDtypeStruct((half, 2 * width), bf16)] * (2 * len(chunks)),
        compiler_params=pltpu.CompilerParams(vmem_limit_bytes=24 << 20),
        cost_estimate=cost(brief * 8 * count * depth * width, brief * (8 * depth * width + 12 * count * width)),
        name="twin_products",
    )(rows, gate_rows, up_rows, *after)


def hop(outer, inv_in, stream, t, got_e, got_m, part_out, part_in, after):
    half = part_out[0].shape[0]
    count = len(stream)

    def inside(j):
        return 0 <= j < count

    def columns(*js):
        return max([stream[j].columns for j in js if inside(j)], default=0)

    def wide(*js):
        return max([stream[j].width for j in js if inside(j)], default=0)

    def hid_e(step):
        return inside(step - 3) or inside(step - 5)

    names, operands, specs = ["outer"], [outer], [SMEM]

    def add(name, value):
        names.append(name)
        operands.append(value)
        specs.append(VMEM)

    if columns(t, t - 2) or hid_e(t):
        add("got_e", got_e)
    if got_m is not None and (inside(t - 1) or inside(t - 4)):
        add("got_m", got_m)
    if inside(t + 1):
        add("next_out", part_out[t + 1])
    if inside(t):
        add("out", part_out[t])
    if inside(t - 1):
        add("in1", part_in[t - 1])
    starts_inv = inside(t - 2) and stream[t - 2].columns > stream[t - 2].pair
    if inside(t - 2):
        add("in2", part_in[t - 2])
        if not starts_inv:
            add("inv", inv_in)
    operands += after
    specs += [ANY] * len(after)
    nxt = t + 1
    hid_at_e = columns(nxt, nxt - 2)
    hid_at_got_e = columns(t, t - 2)
    width_e = hid_at_e + wide(nxt - 3, nxt - 5)
    hid_at_m = columns(t)
    hid_at_got_m = columns(t - 1)
    width_m = hid_at_m + wide(t - 3)
    widths = [w for w in (width_e, width_m) if w]

    def kernel(*refs):
        r = dict(zip(names, refs))
        outs = list(refs[len(operands) :])
        to_e = outs.pop(0) if width_e else None
        to_m = outs.pop(0) if width_m else None

        def both(own, received, to, j):
            pair, end = stream[j].pair, stream[j].columns
            to[:, :pair] = (own[:, :pair].astype(f32) + received[:, :pair].astype(f32)).astype(bf16)
            if end > pair:
                to[:, pair:end] = add_in_three(own[:, pair:], received[:, pair:end])[1]

        @pl.when(r["outer"][0] != 0)
        def _():
            if inside(t + 1):
                pair = stream[t + 1].pair
                to_e[:, :pair] = r["next_out"][:, :pair]
            if inside(t - 2):
                w, pair = stream[t - 2].width, stream[t - 2].pair
                if starts_inv:
                    squares, _ = add_in_three(r["in2"][:, pair:], r["got_e"][:, pair : pair + LANES])
                    inv = lax.rsqrt(squares / D + eps)
                    outs[0][...] = inv
                else:
                    inv = r["inv"][...]
                gate = (r["in2"][:, :w].astype(f32) + r["got_e"][:, :w].astype(f32)) * inv
                up = (r["in2"][:, w:pair].astype(f32) + r["got_e"][:, w:pair].astype(f32)) * inv
                to_e[:, hid_at_e : hid_at_e + w] = (gate / (1.0 + jnp.exp(-gate)) * up).astype(bf16)

        @pl.when(r["outer"][0] == 0)
        def _():
            if inside(t - 1):
                both(r["in1"], r["got_m"], to_e, t - 1)
            if inside(t - 4):
                w = stream[t - 4].width
                to_e[:, hid_at_e : hid_at_e + w] = r["got_m"][:, hid_at_got_m : hid_at_got_m + w]
            if inside(t):
                both(r["out"], r["got_e"], to_m, t)
            if inside(t - 3):
                w = stream[t - 3].width
                to_m[:, hid_at_m : hid_at_m + w] = r["got_e"][:, hid_at_got_e : hid_at_got_e + w]
            if starts_inv:
                outs[0][...] = jnp.zeros(outs[0].shape, f32)

    shapes = [jax.ShapeDtypeStruct((half, w), bf16) for w in widths]
    if starts_inv:
        shapes.append(jax.ShapeDtypeStruct((half, 1), f32))
    outs = pl.pallas_call(
        kernel,
        in_specs=specs,
        out_specs=[VMEM] * len(shapes),
        out_shape=shapes,
        compiler_params=pltpu.CompilerParams(vmem_limit_bytes=24 << 20),
        cost_estimate=cost(16 * half * WIDTH, 20 * half * WIDTH),
        name="hop",
    )(*operands)
    outs = list(outs)
    to_e = (outs.pop(0), hid_at_e) if width_e else None
    to_m = (outs.pop(0), hid_at_m) if width_m else None
    return to_e, to_m, outs[0] if outs else inv_in


def hidden_rows(outer, width, buffers, after):
    half = buffers[0][0].shape[0]

    def kernel(outer_ref, sent, got, from_m, late, *rest):
        hid = rest[-1]

        @pl.when(outer_ref[0] != 0)
        def _():
            hid[:half] = late[:, buffers[3][1] : buffers[3][1] + width]
            hid[half:] = sent[:, buffers[0][1] : buffers[0][1] + width]

        @pl.when(outer_ref[0] == 0)
        def _():
            hid[:half] = from_m[:, buffers[2][1] : buffers[2][1] + width]
            hid[half:] = got[:, buffers[1][1] : buffers[1][1] + width]

    return pl.pallas_call(
        kernel,
        in_specs=[SMEM] + [VMEM] * 4 + [ANY] * len(after),
        out_specs=VMEM,
        out_shape=jax.ShapeDtypeStruct((2 * half, width), bf16),
        compiler_params=pltpu.CompilerParams(vmem_limit_bytes=24 << 20),
        name="hidden_rows",
    )(outer, *[buffer for buffer, _ in buffers], *after)


def down_product(total, chunk, hidden, w_down):
    weight = w_down[chunk.first : chunk.first + chunk.units]
    term = jnp.dot(hidden[:, : chunk.units], weight, preferred_element_type=f32)
    return term if total is None else total + term


def mlp_line(scaled, w_gate, w_up, w_down):
    place = lax.axis_index("mix")
    left = place < 2
    outer = ((place == 0) | (place == 3)).astype(jnp.int32).reshape(1)

    across = [swap(part, "ffn") for part in scaled]
    beside = [swap(part, "pair") for part in scaled]
    diagonal = [swap(part, "pair") for part in across]
    here = jnp.concatenate(scaled + across)
    there = jnp.concatenate(beside + diagonal)
    rows = jnp.concatenate([jnp.where(left, here, there), jnp.where(left, there, here)])
    half = here.shape[0]

    gate_rows = pltpu.with_memory_space_constraint(w_gate.T, pltpu.HBM)
    up_rows = pltpu.with_memory_space_constraint(w_up.T, pltpu.HBM)
    chunks = chunks_of(gate_rows.shape[0])
    streams = (chunks[0::2], chunks[1::2])
    part_out, part_in = ({}, {}), ({}, {})
    sent, got = {}, {}

    def products(k, after):
        if k >= len(chunks) or k // 2 in part_out[k % 2]:
            return after
        if k >= 2 and k % 2 == 0 and k + 1 < len(chunks) and chunks[k + 1].units == chunks[k].width:
            made = twin_products(chunks[k : k + 2], rows, gate_rows, up_rows, after)
            part_out[1][k // 2], part_in[1][k // 2] = made[2:]
        else:
            made = partial_products(chunks[k], rows, gate_rows, up_rows, after)
        part_out[k % 2][k // 2], part_in[k % 2][k // 2] = made[:2]
        return [made[0]]

    def send(s, t, to_e, to_m):
        sent["e", s, t], sent["m", s, t] = to_e, to_m
        got["e", s, t] = (outward(to_e[0]), to_e[1]) if to_e else None
        got["m", s, t] = (middle(to_m[0]), to_m[1]) if to_m else None

    def hidden_of(k):
        s, j = k % 2, k // 2
        return [sent["e", s, j + 3], got["e", s, j + 3], got["m", s, j + 4], got["e", s, j + 5]]

    after = products(0, [])
    send(0, 0, (part_out[0][0], 0), None)
    after = products(1, after)
    send(1, 0, (part_out[1][0], 0), None)
    after = products(2, after)
    total, inv_in, totals = None, None, []
    for t in range(len(streams[0]) + 5):
        for s in (0, 1):
            count = len(streams[s])
            if t < count + 4:
                got_e, got_m = got["e", s, t], got["m", s, t]
                to_e, to_m, inv_in = hop(
                    outer,
                    inv_in,
                    streams[s],
                    t,
                    got_e and got_e[0],
                    got_m and got_m[0],
                    part_out[s],
                    part_in[s],
                    after,
                )
                send(s, t + 1, to_e, to_m)
                after = [(to_e or to_m)[0]]
            k = 2 * t + s + 3
            if k < len(chunks) and k // 2 in part_out[k % 2]:
                k += 1
            after = products(k, after)
            if 0 <= t - 5 < count:
                k = 2 * (t - 5) + s
                earlier = totals[-2:-1] if t > len(streams[0]) else totals[-1:]
                hidden = hidden_rows(outer, chunks[k].width, hidden_of(k), after + earlier)
                total = down_product(total, chunks[k], hidden, w_down)
                totals.append(total)
                after = [hidden]
    total = total.astype(bf16)
    far, near = total[:half], total[half:]
    for_here = jnp.where(left, far, near)
    for_there = jnp.where(left, near, far)
    chip = for_here.astype(f32) + swap(for_there, "pair").astype(f32)
    block = half // 2
    return chip[:block] + swap(chip[block:].astype(bf16), "ffn").astype(f32)


def mlp_sums(normed, w_gate, w_up, w_down):
    gathered = lax.all_gather(normed, ("ffn", "pair"), axis=0, tiled=True)
    parts = []
    for weight in (w_gate, w_up):
        part = jnp.dot(gathered, weight, preferred_element_type=jnp.float32).astype(jnp.bfloat16)
        parts.append(lax.psum_scatter(part, "mix", scatter_dimension=0, tiled=True).astype(jnp.float32))
    hidden = (jax.nn.silu(parts[0]) * parts[1]).astype(jnp.bfloat16)
    hidden = lax.all_gather(hidden, "mix", axis=0, tiled=True)
    partial_value = jnp.dot(hidden, w_down, preferred_element_type=jnp.float32)
    return lax.psum_scatter(
        partial_value.astype(jnp.bfloat16), ("ffn", "pair"), scatter_dimension=0, tiled=True
    ).astype(jnp.float32)


def per_device(
    on_line,
    query,
    new_key,
    new_value,
    key_cache,
    value_cache,
    lengths,
    counts,
    residual,
    norm_gain,
    w_gate,
    w_up,
    w_down,
):
    if on_line:
        xs, scaled, after = [], [], []
        for part in range(PARTS):
            x, ready = attend_rows(
                part,
                PARTS,
                query,
                new_key,
                new_value,
                key_cache,
                value_cache,
                lengths,
                residual,
                norm_gain,
                after,
            )
            xs.append(x)
            scaled.append(ready)
            after = [ready]
        x = jnp.concatenate(xs)
        mlp = mlp_line(scaled, w_gate, w_up, w_down)
    else:
        x = residual.astype(f32) + attend(query, new_key, new_value, key_cache, value_cache, lengths)
        inv = lax.rsqrt(lax.psum(jnp.sum(x * x, axis=1, keepdims=True), "mix") / D + eps)
        normed = (x * inv * norm_gain.astype(f32)).astype(bf16)
        mlp = mlp_sums(normed, w_gate, w_up, w_down)
    slots = jnp.arange(x.shape[0], dtype=jnp.int32)
    live = slots < counts[0]
    return jnp.where(live[:, None], x + mlp, jnp.zeros_like(x)).astype(jnp.bfloat16)


def solution(mesh):
    sizes = mesh.shape
    on_line = sizes["mix"] == 4 and sizes["ffn"] == 2 and sizes["pair"] == 2
    placed = (
        P(("grp", "ffn", "pair"), "mix"),
        P(("grp", "ffn", "pair"), "mix"),
        P(("grp", "ffn", "pair"), "mix"),
        P(("grp", "ffn", "pair"), None, "mix"),
        P(("grp", "ffn", "pair"), None, "mix"),
        P(("grp", "ffn", "pair")),
        P(("grp", "ffn", "pair")),
        P(("grp", "ffn", "pair"), "mix"),
        P("mix"),
        P("mix", ("ffn", "pair")),
        P("mix", ("ffn", "pair")),
        P(("ffn", "pair"), "mix"),
    )
    return jax.shard_map(
        functools.partial(per_device, on_line),
        mesh=mesh,
        in_specs=placed,
        out_specs=P(("grp", "ffn", "pair"), "mix"),
        check_vma=False,
    )
```
